32 devices in a mesh: group: 8 (over z, x), batch: 4 (over y, core).
Axes of the slice: x: 2, y: 2, z: 4, core: 2. Of those that a mesh axis runs over, the one named last changes fastest.
Arguments:
- mixed_input: bfloat16 [8192, 2816], P(('batch', 'group')), parts along dimension 0, may hold values from -6 to 6
- conv_weight: float32 [4, 2816], replicated, may hold values from -3 to 3
- conv_bias: float32 [2816], replicated, may hold values from -3 to 3
- gate_input: bfloat16 [8192, 2560], P(('batch', 'group')), parts along dimension 0, may hold values from -6 to 6
- log_decay: float32 [40, 8192], P(None, ('batch', 'group')), parts along dimension 1, may hold values from -0.76 to 0, as said below
- level_weights: float32 [40, 20, 8192], P(None, None, ('batch', 'group')), parts along dimension 2, may hold values from 0.2 to 2
- skip_gain: float32 [40], replicated, may hold values from 0.3 to 3
- norm_gain: float32 [2560], replicated, may hold values from 0.25 to 1.75
- seg_lengths: int32 [12], P('batch'), parts along dimension 0, may hold values from 1 to 1280, 2048 in all
Outputs:
- output: bfloat16 [8192, 2560], P(('batch', 'group')), parts along dimension 0
The draws below stay inside these ranges and needn't reach their ends.
There are 4 independent parts, one for each index of `batch`. The reference program is written for one: setup_inputs(seed, part) draws one part's arguments, and reference() takes and returns one part's arrays. A program takes and returns all parts, laid end to end along the dimension named above; an argument that names none is the same for every part. Nothing has to cross between parts.
Inputs may be any that keep to these rules, and one draw needn't show every extreme that they name: `seg_lengths`: the recordings' lengths in order; they sum to 2048 and the longest is exactly 1280. `log_decay`: every entry is negative.
All inputs are finite; a program needn't handle non-finite values.
Results may differ from the reference program's by a relative error of at most 0.0034.
Values may be sent and summed in bfloat16 or wider, within the bound.
No kernel may reach another device: no remote copies, remote signals or barrier semaphores. Data moves between devices by JAX's collectives and lax.ppermute only.
A program may use at most 128 MiB of HBM per device.

```python
import math
import jax
import jax.numpy as jnp
import numpy as np
from jax import lax

WIDTH = 2560
ATTENTION_UNITS = 40
HEAD_DIM = 64
STATE = 128
KERNEL = 4
LEVELS = 20
SEGS = 3
TOK_DEV = 256
RECORD_POSITIONS = 2048
CONV_CH = 2816
LONG = 1280


def draw_log_decay(key, part):
    addressing_vectors = jax.random.split(key, 6)
    fast_share = 0.5
    rough_lo = 0.5
    rough_hi = 1.5
    fast = jax.random.uniform(addressing_vectors[0], (ATTENTION_UNITS,), jnp.float32) < fast_share
    fast_rate = jnp.exp(jax.random.uniform(addressing_vectors[1], (ATTENTION_UNITS,), jnp.float32, jnp.log(1.0 / 50.0), jnp.log(1.0 / 30.0)))
    slow_rate = jnp.exp(jax.random.uniform(addressing_vectors[2], (ATTENTION_UNITS,), jnp.float32, jnp.log(0.03 / RECORD_POSITIONS), jnp.log(0.3 / RECORD_POSITIONS)))
    forgetting_speed = jnp.where(fast, fast_rate, slow_rate)
    rough_approximation = jax.random.uniform(addressing_vectors[3], (ATTENTION_UNITS, RECORD_POSITIONS), jnp.float32, rough_lo, rough_hi)
    echo_train = jax.random.uniform(addressing_vectors[4], (ATTENTION_UNITS, RECORD_POSITIONS), jnp.float32) < 4.0 / RECORD_POSITIONS
    fitting_objective = jnp.log(jax.random.uniform(addressing_vectors[5], (ATTENTION_UNITS, RECORD_POSITIONS), jnp.float32, 0.5, 0.8))
    return (-forgetting_speed[:, None] * rough_approximation + jnp.where(echo_train, fitting_objective, 0.0)).astype(jnp.float32)


def block_levels(key, extent, shards, least, high):
    level = 1.0
    for axis_at, blocks in shards:
        heights = jax.random.uniform(jax.random.fold_in(jax.random.fold_in(key, 6), axis_at), (blocks,), jnp.float32, least / len(shards), high / len(shards))
        level = level * jnp.repeat(jnp.exp(heights), extent[axis_at] // blocks).reshape((-1,) + (1,) * (len(extent) - 1 - axis_at))
    return level


def split_up(count, total, limit, slope):
    loads = [(1 << 20) // math.isqrt(grade ** slope) + 1 for grade in range(2, count + 1)]
    rest, given = total - limit - (count - 1), [1] * (count - 1)
    while rest > 0:
        movable = [i for i in range(count - 1) if given[i] < limit]
        pool, remaining = sum([loads[i] for i in movable]), rest
        for i in movable:
            addition = min(limit - given[i], max(1, remaining * loads[i] // pool), rest)
            given[i] = given[i] + addition
            rest = rest - addition
    return np.array([limit] + given)


def uneven(stream_key, number_of, total, bound, lean):
    if number_of == 2:
        one = jax.random.randint(stream_key, (), max(1, total - bound), min(bound, total - 1) + 1)
        return jnp.stack([one, total - one])
    sizes = jnp.asarray(split_up(number_of, total, bound, lean), jnp.int32)
    couples = (number_of - 1) // 2
    donor, receiver = sizes[1:1 + 2 * couples:2], sizes[2:2 + 2 * couples:2]
    margin = jnp.minimum(donor - 1, bound - receiver)
    passed = jax.random.randint(jax.random.fold_in(stream_key, 1), (couples,), 0, 1 << 20) % (margin + 1)
    sizes = sizes.at[1:1 + 2 * couples:2].set(donor - passed).at[2:2 + 2 * couples:2].set(receiver + passed)
    return sizes[jax.random.permutation(jax.random.fold_in(stream_key, 2), number_of)]


def bell_draw(key, extent, width, limit, cuts=(), kind=jnp.bfloat16):
    values = width * jax.random.normal(key, extent, jnp.float32)
    if cuts:
        values = values * block_levels(key, extent, cuts, -0.22, 0.18)
    return jnp.clip(values, -limit, limit).astype(kind)


def setup_inputs(seed: int = 0, part: int = 0) -> dict:
    key_of = jax.random.split(jax.random.key(seed), 10)
    own_keys = jax.random.split(jax.random.fold_in(key_of[9], part), 10)
    mixed_input = bell_draw(own_keys[0], (RECORD_POSITIONS, CONV_CH), 1.0, 6.0, ((0, 8),))
    conv_weight = bell_draw(key_of[1], (KERNEL, CONV_CH), KERNEL ** -0.5, 3.0, (), jnp.float32)
    conv_bias = bell_draw(key_of[2], (CONV_CH,), 0.5, 3.0, (), jnp.float32)
    gate_input = bell_draw(own_keys[3], (RECORD_POSITIONS, WIDTH), 1.0, 6.0, ((0, 8),))
    log_decay = draw_log_decay(jax.random.fold_in(jax.random.fold_in(key_of[9], part), 71), part)
    level_weights = jnp.clip(jnp.exp(math.log(2.0) - 2.3025851 * jax.random.uniform(own_keys[5], (ATTENTION_UNITS, LEVELS, RECORD_POSITIONS), jnp.float32) ** block_levels(own_keys[5], (ATTENTION_UNITS, LEVELS, RECORD_POSITIONS), ((2, 8),), -0.2, 0.2)), 0.2, 2.0)
    skip_gain = jnp.clip(jnp.exp(jax.random.uniform(key_of[6], (ATTENTION_UNITS,), jnp.float32, math.log(0.3), math.log(3.0))), 0.3, 3.0)
    norm_gain = jnp.clip(1.0 + 0.15 * jax.random.normal(key_of[7], (WIDTH,), jnp.float32), 0.25, 1.75)
    seg_lengths = uneven(own_keys[8], SEGS, RECORD_POSITIONS, LONG, 0).astype(jnp.int32)
    return {"mixed_input": mixed_input, "conv_weight": conv_weight, "conv_bias": conv_bias, "gate_input": gate_input, "log_decay": log_decay, "level_weights": level_weights, "skip_gain": skip_gain, "norm_gain": norm_gain, "seg_lengths": seg_lengths}


def segment_of(positions, seg_lengths):
    bounds = jnp.cumsum(seg_lengths)[:-1].astype(jnp.int32)
    found = lax.optimization_barrier(jnp.sum((positions[:, None] >= bounds[None, :]).astype(jnp.int32), axis=1)).astype(jnp.int32)
    return jnp.where(positions >= 0, found, -1).astype(jnp.int32)

def pair_levels(count, low_bits):
    index = jnp.arange(count, dtype=jnp.int32)
    diff = jnp.bitwise_xor(index[:, None], index[None, :])
    levels = jnp.zeros((count, count), jnp.int32)
    for bit_index in range(low_bits):
        levels = levels + (diff >= 2 ** bit_index).astype(jnp.int32)
    return levels

def convolve(rows, segs, conv_weight, conv_bias, taps):
    count = rows.shape[0] - (taps - 1)
    total = jnp.zeros((count, rows.shape[1]), jnp.float32) + conv_bias[None, :]
    for tap in range(taps):
        begin = taps - 1 - tap
        piece = rows[begin:begin + count].astype(jnp.float32)
        same = (segs[begin:begin + count] == segs[taps - 1:]).astype(jnp.float32)
        total = total + conv_weight[tap][None, :] * piece * same[:, None]
    return jax.nn.silu(total)

def reference(mixed_input, conv_weight, conv_bias, gate_input, log_decay, level_weights, skip_gain, norm_gain, seg_lengths):
    tok_rows = TOK_DEV
    group_count = RECORD_POSITIONS // tok_rows
    low_bits = tok_rows.bit_length() - 1
    high_bits = group_count.bit_length() - 1
    head_count = ATTENTION_UNITS
    head_dim = HEAD_DIM
    positions = jnp.arange(RECORD_POSITIONS, dtype=jnp.int32)
    segs = segment_of(positions, seg_lengths)
    padded_rows = jnp.concatenate([jnp.zeros((KERNEL - 1, CONV_CH), mixed_input.dtype), mixed_input], axis=0)
    padded_segs = jnp.concatenate([jnp.full((KERNEL - 1,), -1, jnp.int32), segs], axis=0)
    activated = convolve(padded_rows, padded_segs, conv_weight, conv_bias, KERNEL)
    xs = activated[:, :WIDTH].astype(jnp.bfloat16)
    keys = activated[:, WIDTH:WIDTH + STATE].astype(jnp.bfloat16)
    queries = activated[:, WIDTH + STATE:].astype(jnp.bfloat16)
    cum = jnp.cumsum(log_decay.reshape(head_count, group_count, tok_rows), axis=2)
    seg_groups = segs.reshape(group_count, tok_rows)
    last_seg = seg_groups[:, -1]
    prev_seg = jnp.concatenate([jnp.full((1,), -1, jnp.int32), last_seg[:-1]])
    through = jnp.exp(cum[:, :, -1]).T * (last_seg == prev_seg).astype(jnp.float32)[:, None]
    x_groups = xs.reshape(group_count, tok_rows, head_count, head_dim)
    k_groups = keys.reshape(group_count, tok_rows, STATE)
    q_groups = queries.reshape(group_count, tok_rows, STATE)
    cum_groups = jnp.transpose(cum, (1, 0, 2))
    lam_groups = jnp.transpose(level_weights.reshape(head_count, LEVELS, group_count, tok_rows), (2, 0, 1, 3))
    gate_groups = gate_input.reshape(group_count, tok_rows, WIDTH)

    def end_state(items):
        x_part, k_part, cum_part, seg_part = items
        same = (seg_part == seg_part[-1]).astype(jnp.float32)
        weight = jnp.exp(cum_part[:, -1:] - cum_part) * same[None, :]
        scaled = (x_part.astype(jnp.float32) * weight.T[:, :, None]).astype(jnp.bfloat16)
        return jnp.einsum('sn,shp->hnp', k_part.astype(jnp.float32), scaled.astype(jnp.float32))
    states = lax.map(end_state, (x_groups, k_groups, cum_groups, seg_groups))
    pair_level = pair_levels(tok_rows, low_bits)
    row_ids = jnp.arange(tok_rows, dtype=jnp.int32)
    lower_tri = row_ids[None, :] <= row_ids[:, None]
    group_ids = jnp.arange(group_count, dtype=jnp.int32)

    def one_group(items):
        index, x_part, k_part, q_part, cum_part, seg_part, lam_part, gate_part, prev_part = items
        scores = jnp.dot(q_part, k_part.T, preferred_element_type=jnp.float32)
        valid = lower_tri & (seg_part[:, None] == seg_part[None, :])
        gap = jnp.where(valid[None], cum_part[:, :, None] - cum_part[:, None, :], 0.0)
        decay = jnp.exp(gap) * valid[None].astype(jnp.float32)
        picked = jnp.transpose(lam_part, (0, 2, 1))[:, row_ids[:, None], pair_level]
        mixing = lax.optimization_barrier((scores[None] * picked * decay).astype(jnp.bfloat16))
        result = jnp.einsum('hts,shp->thp', mixing.astype(jnp.float32), x_part.astype(jnp.float32))
        alive = (seg_part == prev_part).astype(jnp.float32)
        entry = jnp.exp(cum_part) * alive[None, :]
        open_through = jnp.where((group_ids < index)[:, None], through, 1.0)
        carried = jnp.cumprod(open_through[::-1], axis=0)[::-1]
        suffix = jnp.concatenate([carried[1:], jnp.ones((1, head_count), jnp.float32)], axis=0)
        for bit_index in range(high_bits):
            size = 2 ** bit_index
            is_set = index // size % 2 == 1
            first = index // (2 * size) * (2 * size)
            inside = (group_ids >= first) & (group_ids < first + size) & is_set
            weights = jnp.where(inside[:, None], suffix, 0.0)
            level_state = jnp.einsum('jh,jhnp->hnp', weights, states, precision=lax.Precision.HIGHEST)
            level_half = lax.optimization_barrier(level_state.astype(jnp.bfloat16))
            read = jnp.einsum('tn,hnp->thp', q_part.astype(jnp.float32), level_half.astype(jnp.float32))
            coef = lam_part[:, low_bits + 1 + bit_index, :] * entry
            result = result + read * coef.T[:, :, None]
        result = result + skip_gain[None, :, None] * x_part.astype(jnp.float32)
        flat = result.reshape(tok_rows, WIDTH)
        gated = flat * jax.nn.silu(gate_part.astype(jnp.float32))
        scale = lax.rsqrt(lax.optimization_barrier(jnp.mean(gated * gated, axis=1, keepdims=True)) + 1e-05)
        return (gated * scale * norm_gain[None, :]).astype(jnp.bfloat16)
    output = lax.map(one_group, (group_ids, x_groups, k_groups, q_groups, cum_groups, seg_groups, lam_groups, gate_groups, prev_seg))
    return output.reshape(RECORD_POSITIONS, WIDTH)
```

```python
import functools

import jax
import jax.numpy as jnp
from jax import lax
from jax.experimental import pallas as pl
from jax.experimental.pallas import tpu as pltpu
from jax.sharding import PartitionSpec as P

eps_norm = 1e-05
bf16 = jnp.bfloat16
f32 = jnp.float32
HALO = 16
PLACES = 4
LANES = 128
EXACT = lax.Precision.HIGHEST


def iota(shape, dim):
    return lax.broadcasted_iota(jnp.int32, shape, dim)


def dot(a, b, contract, precision=None):
    return lax.dot_general(
        a, b, (contract, ((), ())), precision=precision, preferred_element_type=f32
    )


def silu(v):
    return v * (0.5 * jnp.tanh(0.5 * v) + 0.5)


def segment_bounds(info, recordings):
    bounds, total = [], 0
    for index in range(recordings - 1):
        total = total + info[index]
        bounds.append(total)
    return bounds


def segment_of(pos, bounds):
    found = jnp.where(pos >= 0, 0, -1)
    for bound in bounds:
        found = found + jnp.where(pos >= bound, 1, 0)
    return found


def same_segment(pos, other, bounds):
    return (segment_of(pos, bounds) == segment_of(other, bounds)).astype(f32)


def two_parts(value):
    high = value.astype(bf16).astype(f32)
    return high, value - high


def spread(rows, first_head, columns, head_dim, repeats):
    row = lax.rem(iota((rows * repeats, columns), 0), rows)
    head = first_head + iota((rows * repeats, columns), 1) // head_dim
    return (row == head).astype(bf16)


def conv_taps(shifts, weight_ref, bias_ref, lo, hi):
    total = bias_ref[0:1, lo:hi]
    for tap, piece in enumerate(shifts):
        total = total + weight_ref[tap : tap + 1, lo:hi] * piece
    return silu(total)


def features_kernel(
    dims, info, x_ref, kq_in_ref, w_ref, b_ref, wkq_ref, bkq_ref, decay_ref,
    xs_ref, kq_ref, part_ref, cum_ref, cumt_ref, ewt_ref, same_ref, keys_ref,
):
    tok, heads, head_dim, taps, recordings, block = dims
    state = keys_ref.shape[0]
    step = pl.program_id(0)

    def features(rows_ref, weight_ref, bias_ref):
        width = rows_ref.shape[1]
        halves = []
        for lo in range(0, width, LANES):
            x = rows_ref[:, lo : lo + LANES].astype(f32)
            shifts = [x] + [
                pltpu.roll(x, tap, 0) * same_ref[tap - 1] for tap in range(1, taps)
            ]
            halves.append(conv_taps(shifts, weight_ref, bias_ref, lo, lo + LANES))
        return jnp.concatenate(halves, axis=1)

    @pl.when(step == 0)
    def _():
        bounds = segment_bounds(info, recordings)
        first = info[recordings] * tok
        pos = first + iota((tok, LANES), 0)
        for tap in range(1, taps):
            same_ref[tap - 1] = same_segment(pos, pos - tap, bounds)
        decay = jnp.concatenate(
            [decay_ref[...], jnp.zeros((LANES - heads, tok), f32)], axis=0
        )
        upper = (iota((tok, tok), 0) <= iota((tok, tok), 1)).astype(f32)
        lower = (iota((tok, tok), 0) >= iota((tok, tok), 1)).astype(f32)
        cum_ref[...] = dot(decay_ref[...], upper, ((1,), (0,)), EXACT)
        cumt = dot(lower, decay, ((1,), (1,)), EXACT)
        cumt_ref[...] = cumt
        end = cumt[tok - 1 : tok, :]
        ewt_ref[...] = jnp.exp(end - cumt) * same_segment(
            pos, jnp.zeros_like(pos) + (first + tok - 1), bounds
        )
        kq = features(kq_in_ref, wkq_ref, bkq_ref)
        kq_ref[...] = kq.astype(bf16)
        keys = jnp.transpose(kq[:, :state])
        keys_ref[...] = jnp.where(iota((state, tok), 1) >= HALO, keys, 0.0).astype(bf16)

    xs = features(x_ref, w_ref, b_ref).astype(bf16)
    xs_ref[...] = xs
    high, low = two_parts(ewt_ref[...])
    weight = dot(
        jnp.concatenate([high, low], axis=1).astype(bf16),
        spread(LANES, step * (block // head_dim), block, head_dim, 2),
        ((1,), (0,)),
    )
    scaled = (xs.astype(f32) * weight).astype(bf16)
    part_ref[...] = dot(keys_ref[...], scaled, ((1,), (0,)))


def join_kernel(
    dims, info, halo_ref, head_ref, w_ref, b_ref, ewt_ref, cumt_ref, part_ref,
    px_ref, pkq_ref, own_ref, one_ref, two_ref, three_ref, rest_ref, scaled_ref,
):
    tok, heads, head_dim, taps, recordings, width, state = dims
    bounds = segment_bounds(info, recordings)
    group = info[recordings]
    first = group * tok
    pos = first + iota((HALO, LANES), 0)
    same = [same_segment(pos, pos - tap, bounds) for tap in range(1, taps)]
    high, low = two_parts(ewt_ref[...])
    split = jnp.concatenate([high, low], axis=1).astype(bf16)

    def features(lo):
        hi = lo + LANES
        both = jnp.concatenate(
            [halo_ref[:, lo:hi].astype(f32), head_ref[:, lo:hi].astype(f32)], axis=0
        )
        shifts = [both[HALO:]] + [
            pltpu.roll(both, tap, 0)[HALO:] * same[tap - 1] for tap in range(1, taps)
        ]
        return conv_taps(shifts, w_ref, b_ref, lo, hi)

    keys = None
    for lo in range(width, width + 2 * state, LANES):
        part = features(lo).astype(bf16)
        pkq_ref[:, lo - width : lo - width + LANES] = part
        if lo == width:
            keys = part
    block = 4 * LANES
    for lo in range(0, width, block):
        xs = jnp.concatenate(
            [features(lo + at) for at in range(0, block, LANES)], axis=1
        ).astype(bf16)
        px_ref[:, lo : lo + block] = xs
        weight = dot(
            split, spread(LANES, lo // head_dim, block, head_dim, 2), ((1,), (0,))
        )
        scaled_ref[:, lo : lo + block] = (xs.astype(f32) * weight).astype(bf16)

    end = cumt_ref[HALO - 1 : HALO, :]
    alive = same_segment(first + tok - 1 + 0 * pos[:1], first - 1 + 0 * pos[:1], bounds)
    through = jnp.exp(end) * alive
    high, rest = two_parts(through)
    mid, low = two_parts(rest)
    row = iota((HALO, LANES), 0)
    tail = jnp.where(row == 0, high, jnp.where(row == 1, mid, jnp.where(row == 2, low, 0.0)))
    place = lax.rem(group, PLACES)
    cols = width // PLACES
    for mask, out_ref in enumerate((own_ref, one_ref, two_ref, three_ref)):
        where = pl.multiple_of(jnp.bitwise_xor(place, mask) * cols, LANES)
        value = part_ref[:, pl.ds(where, cols)] + dot(
            keys, scaled_ref[:, pl.ds(where, cols)], ((0,), (0,))
        )
        value = value.astype(bf16)
        out_ref[:state, :] = value
        out_ref[state:, :LANES] = tail.astype(bf16)
        out_ref[state:, LANES:] = jnp.zeros((HALO, cols - LANES), bf16)
        if mask != 1:
            rest_ref[max(mask - 1, 0)] = value


def combine_kernel(
    dims, info, own_ref, one_ref, two_ref, three_ref, quad_ref, pair_ref, scale_ref
):
    state, head_dim, recordings = dims
    cols = quad_ref.shape[1]
    place = lax.rem(info[recordings], PLACES)
    refs = (own_ref, one_ref, two_ref, three_ref)
    got = []
    for ref in refs:
        tail = ref[state:, :LANES].astype(f32)
        got.append(tail[0:1] + tail[1:2] + tail[2:3])
    through = []
    for at in range(PLACES):
        total = jnp.zeros((1, LANES), f32)
        for mask in range(PLACES):
            total = total + jnp.where(jnp.bitwise_xor(place, mask) == at, got[mask], 0.0)
        through.append(total)
    ones = jnp.ones((1, LANES), f32)
    rows = []
    for mask in range(PLACES):
        at = jnp.bitwise_xor(place, mask)
        product = ones
        for later in range(1, PLACES):
            product = product * jnp.where(later > at, through[later], ones)
        rows.append(product)
    for mask in range(PLACES):
        at = jnp.bitwise_xor(place, mask)
        rows.append(jnp.where(at == 0, through[1], jnp.where(at == 1, ones, 0.0 * ones)))
    before_quad = ones
    for earlier in range(PLACES - 1):
        before_quad = before_quad * jnp.where(earlier < place, through[earlier], ones)
    everything = through[0] * through[1] * through[2] * through[3]
    row = iota((8, LANES), 0)
    scale = jnp.where(row == 1, jnp.where(place == 3, through[2], ones), ones)
    scale = jnp.where(row == 2, before_quad, scale)
    scale_ref[...] = jnp.where(row == 3, everything, scale)
    weights = jnp.concatenate(rows, axis=0)
    high, low = two_parts(weights)
    weights = dot(
        jnp.concatenate([high, low], axis=1).astype(bf16),
        spread(LANES, place * (cols // head_dim), cols, head_dim, 2),
        ((1,), (0,)),
    )
    quad = jnp.zeros((state, cols), f32)
    pair = jnp.zeros((state, cols), f32)
    for mask, ref in enumerate(refs):
        value = ref[:state, :].astype(f32)
        quad = quad + value * weights[mask : mask + 1]
        pair = pair + value * weights[PLACES + mask : PLACES + mask + 1]
    quad_ref[...] = quad.astype(bf16)
    pair_ref[...] = pair.astype(bf16)


def with_head(patch_ref, body_ref):
    return jnp.concatenate([patch_ref[...], body_ref[HALO:, :]], axis=0)


def local_kernel(
    dims, info, xs_ref, px_ref, kq_ref, pkq_ref, cum_ref, level_ref, skip_ref,
    out_ref, scores_ref, mixing_ref,
):
    tok, head_dim, recordings, state, low_bits = dims
    per_step = cum_ref.shape[0]
    rows = 32
    row_bits = rows.bit_length() - 1

    @pl.when(pl.program_id(0) == 0)
    def _():
        bounds = segment_bounds(info, recordings)
        first = info[recordings] * tok
        kq = with_head(pkq_ref, kq_ref)
        s_pos = iota((tok, tok), 0)
        t_pos = iota((tok, tok), 1)
        valid = same_segment(first + s_pos, first + t_pos, bounds) * (s_pos <= t_pos)
        scores_ref[...] = dot(kq[:, :state], kq[:, state:], ((1,), (1,))) * valid

    xs = with_head(px_ref, xs_ref)
    cum = cum_ref[...]
    cumt = jnp.transpose(cum)
    diff = jnp.bitwise_xor(iota((rows, tok), 0), lax.rem(iota((rows, tok), 1), rows))
    near = jnp.zeros((rows, tok), jnp.int32)
    for bit in range(row_bits):
        near = near + (diff >= 2**bit).astype(jnp.int32)
    token = iota((1, tok), 1) // rows
    pieces = []
    for head in range(per_step):
        levels = level_ref[head]
        inner = jnp.broadcast_to(levels[0:1], (rows, tok))
        for level in range(1, row_bits + 1):
            inner = jnp.where(near == level, levels[level : level + 1], inner)
        for s in range(0, tok, rows):
            at = s // rows
            start = s // LANES * LANES
            outer = jnp.zeros((1, tok), f32)
            apart = jnp.bitwise_xor(token, at)
            for level in range(row_bits + 1, low_bits + 1):
                outer = jnp.where(
                    apart >= 2 ** (level - row_bits - 1), levels[level : level + 1], outer
                )
            picked = jnp.where(token == at, inner, outer)[:, start:]
            gap = cum[head : head + 1, start:] - cumt[s : s + rows, head : head + 1]
            value = jnp.exp(jnp.minimum(gap, 0.0)) * picked
            mixing_ref[s : s + rows, start:] = (
                value * scores_ref[s : s + rows, start:]
            ).astype(bf16)
            if start:
                mixing_ref[s : s + rows, :start] = jnp.zeros((rows, start), bf16)
        x_head = xs[:, head * head_dim : (head + 1) * head_dim].astype(f32)
        xt = jnp.transpose(x_head).astype(bf16)
        pieces.append(dot(xt, mixing_ref[...], ((1,), (0,))))
    skip = skip_ref[...]
    for at in range(0, per_step, 2):
        lo = at * head_dim
        both = jnp.transpose(jnp.concatenate(pieces[at : at + 2], axis=0))
        hi = lo + 2 * head_dim
        out_ref[:, lo:hi] = both + skip[:, lo:hi] * xs[:, lo:hi].astype(f32)


def spread_rows(coef, cols, head_dim, first_head):
    high, low = two_parts(coef)
    heads = coef.shape[0]
    return dot(
        jnp.concatenate([high, low], axis=0).astype(bf16),
        spread(heads, first_head, cols, head_dim, 2),
        ((0,), (0,)),
    )


def far_kernel(
    dims, mask, info, sum_ref, kq_ref, pkq_ref, coef_ref, low_ref, pair_ref, gate_ref,
    out_ref, next_ref,
):
    head_dim, recordings, state = dims
    cols = sum_ref.shape[1]
    place = lax.rem(info[recordings], PLACES)
    first = jnp.bitwise_xor(place, mask) * (cols // head_dim)
    queries = with_head(pkq_ref, kq_ref)[:, state:]
    total = sum_ref[...]
    for bit, ref in enumerate((low_ref, pair_ref)):
        read = dot(queries, ref[:state, :], ((1,), (0,)))
        total = total + read * spread_rows(coef_ref[bit], cols, head_dim, first)
    gate = silu(gate_ref[...].astype(f32))
    out_ref[...] = total * gate
    next_ref[...] = spread_rows(coef_ref[2], cols, head_dim, first) * gate


def final_kernel(dims, count, info, *refs):
    recordings, state = dims
    sums = refs[:PLACES]
    factors = refs[PLACES : 2 * PLACES]
    queries_ref = refs[2 * PLACES]
    states = refs[2 * PLACES + 1 : 3 * PLACES + 1]
    gain_ref, out_ref = refs[3 * PLACES + 1 :]
    place = lax.rem(info[recordings], PLACES)
    cols = sums[0].shape[1]
    queries = queries_ref[...]
    gated, squares = [], 0.0
    for mask in range(PLACES):
        read = dot(queries, states[mask][...], ((1,), (0,)))
        value = sums[mask][...] + read * factors[mask][...]
        gated.append(value)
        squares = squares + jnp.sum(value * value, axis=1, keepdims=True)
    scale = lax.rsqrt(squares / count + eps_norm)
    for mask in range(PLACES):
        where = pl.multiple_of(jnp.bitwise_xor(place, mask) * cols, LANES)
        out_ref[:, pl.ds(where, cols)] = (
            gated[mask] * scale * gain_ref[:, pl.ds(where, cols)]
        ).astype(bf16)


def whole(shape):
    zeros = (0,) * len(shape)
    return pl.BlockSpec(shape, lambda *_: zeros)


def call(kernel, info, operands, in_specs, outs, out_specs, grid, scratch=(), flops=0, mb=64):
    moved = sum(a.size * a.dtype.itemsize for a in operands)
    moved += sum(o.size * o.dtype.itemsize for o in outs)
    return pl.pallas_call(
        kernel,
        grid_spec=pltpu.PrefetchScalarGridSpec(
            num_scalar_prefetch=1,
            grid=grid,
            in_specs=in_specs,
            out_specs=out_specs,
            scratch_shapes=list(scratch),
        ),
        out_shape=outs,
        compiler_params=pltpu.CompilerParams(vmem_limit_bytes=mb * 2**20 * 3 // 4),
        cost_estimate=pl.CostEstimate(
            flops=flops, bytes_accessed=moved, transcendentals=0
        ),
    )(info, *operands)


def shape(dims, dtype):
    return jax.ShapeDtypeStruct(dims, dtype)


def per_device(
    mixed_input,
    conv_weight,
    conv_bias,
    gate_input,
    log_decay,
    level_weights,
    skip_gain,
    norm_gain,
    seg_lengths,
):
    tok, channels = mixed_input.shape
    width = gate_input.shape[1]
    heads = log_decay.shape[0]
    head_dim = width // heads
    state = (channels - width) // 2
    taps = conv_weight.shape[0]
    recordings = seg_lengths.shape[0]
    low_bits = tok.bit_length() - 1
    groups = lax.axis_size("group")
    high_bits = groups.bit_length() - 1
    group = lax.axis_index("group")
    place = group % PLACES
    cols = width // PLACES
    info = jnp.concatenate([seg_lengths, group[None].astype(jnp.int32)])

    def send(value, pairs):
        return lax.ppermute(value, "group", pairs)

    def quad_send(value, mask, wanted=lambda target: True):
        pairs = [(g, g ^ mask) for g in range(groups) if wanted(g ^ mask)]
        return send(value, pairs)

    halo = send(mixed_input[tok - HALO :], [(g, g + 1) for g in range(groups - 1)])

    block = 2 * state
    bias = conv_bias[None, :]
    xs, kq, part, cum, cumt, ewt = call(
        functools.partial(
            features_kernel, (tok, heads, head_dim, taps, recordings, block)
        ),
        info,
        (mixed_input, mixed_input, conv_weight, bias, conv_weight, bias, log_decay),
        [
            pl.BlockSpec((tok, block), lambda i, *_: (0, i)),
            pl.BlockSpec((tok, block), lambda i, *_: (0, width // block)),
            pl.BlockSpec((taps, block), lambda i, *_: (0, i)),
            pl.BlockSpec((1, block), lambda i, *_: (0, i)),
            pl.BlockSpec((taps, block), lambda i, *_: (0, width // block)),
            pl.BlockSpec((1, block), lambda i, *_: (0, width // block)),
            whole(log_decay.shape),
        ],
        [
            shape((tok, width), bf16),
            shape((tok, block), bf16),
            shape((state, width), f32),
            shape((heads, tok), f32),
            shape((tok, LANES), f32),
            shape((tok, LANES), f32),
        ],
        [
            pl.BlockSpec((tok, block), lambda i, *_: (0, i)),
            whole((tok, block)),
            pl.BlockSpec((state, block), lambda i, *_: (0, i)),
            whole((heads, tok)),
            whole((tok, LANES)),
            whole((tok, LANES)),
        ],
        (width // block,),
        [pltpu.VMEM((taps - 1, tok, LANES), f32), pltpu.VMEM((state, tok), bf16)],
        flops=2 * tok * width * state,
    )

    payload = shape((state + HALO, cols), bf16)
    px, pkq, own, one, two, three, rest = call(
        functools.partial(
            join_kernel, (tok, heads, head_dim, taps, recordings, width, state)
        ),
        info,
        (halo, mixed_input, conv_weight, bias, ewt, cumt, part),
        [
            whole((HALO, channels)),
            whole((HALO, channels)),
            whole(conv_weight.shape),
            whole(bias.shape),
            whole((HALO, LANES)),
            pl.BlockSpec((HALO, LANES), lambda i, *_: (tok // HALO - 1, 0)),
            whole(part.shape),
        ],
        [
            shape((HALO, width), bf16),
            shape((HALO, block), bf16),
            payload,
            payload,
            payload,
            payload,
            shape((PLACES - 1, state, cols), bf16),
        ],
        [
            whole((HALO, width)),
            whole((HALO, block)),
            whole(payload.shape),
            whole(payload.shape),
            whole(payload.shape),
            whole(payload.shape),
            whole((PLACES - 1, state, cols)),
        ],
        (1,),
        [pltpu.VMEM((HALO, width), bf16)],
        flops=2 * HALO * width * state,
    )

    got_one = quad_send(one, 1)
    got_two = quad_send(two, 2)
    got_three = quad_send(three, 3)
    quad, pair, scale = call(
        functools.partial(combine_kernel, (state, head_dim, recordings)),
        info,
        (own, got_one, got_two, got_three),
        [whole(payload.shape)] * PLACES,
        [shape((state, cols), bf16), shape((state, cols), bf16), shape((8, LANES), f32)],
        [whole((state, cols)), whole((state, cols)), whole((8, LANES))],
        (1,),
        flops=4 * state * cols,
    )

    befores = [scale[0, :heads], scale[1, :heads], scale[2, :heads]]
    crossed = []
    running, total = quad, scale[3, :heads]
    for bit in range(2, high_bits):
        mask = 2**bit
        last = bit + 1 == high_bits
        far = quad_send(running, mask, lambda target: not last or target & mask)
        crossed.append(far)
        if not last:
            on_top = group // mask % 2 == 1
            far_total = quad_send(total, mask)

            def columns(value):
                mine = lax.dynamic_slice(value, (place * (cols // head_dim),), (cols // head_dim,))
                return jnp.repeat(mine, head_dim)[None, :]

            running = jnp.where(
                on_top,
                far.astype(f32) * columns(total) + running.astype(f32),
                running.astype(f32) * columns(far_total) + far.astype(f32),
            ).astype(bf16)
            befores.append(jnp.where(on_top, far_total * befores[-1], befores[-1]))
            total = total * far_total

    rests = quad_send(rest, 1, lambda target: target & 1)
    lows = [got_one, rests[0], rests[2], rests[1]]
    pairs = [pair] + [
        quad_send(pair, mask, lambda target: target & 2) for mask in range(1, PLACES)
    ]

    def all_quarters(value, bit):
        return [value] + [
            quad_send(value, mask, lambda target: target & 2**bit)
            for mask in range(1, PLACES)
        ]

    per_step = 8
    skip_cols = jnp.repeat(skip_gain, head_dim)[None, :]
    sums = call(
        functools.partial(
            local_kernel, (tok, head_dim, recordings, state, low_bits)
        ),
        info,
        (xs, px, kq, pkq, cum, level_weights, skip_cols),
        [
            pl.BlockSpec((tok, per_step * head_dim), lambda i, *_: (0, i)),
            pl.BlockSpec((HALO, per_step * head_dim), lambda i, *_: (0, i)),
            whole(kq.shape),
            whole(pkq.shape),
            pl.BlockSpec((per_step, tok), lambda i, *_: (i, 0)),
            pl.BlockSpec((per_step,) + level_weights.shape[1:], lambda i, *_: (i, 0, 0)),
            pl.BlockSpec((1, per_step * head_dim), lambda i, *_: (0, i)),
        ],
        [shape((tok, width), f32)],
        [pl.BlockSpec((tok, per_step * head_dim), lambda i, *_: (0, i))],
        (heads // per_step,),
        [pltpu.VMEM((tok, tok), f32), pltpu.VMEM((tok, tok), bf16)],
        flops=2 * heads * tok * tok * head_dim,
    )[0]

    positions = group * tok + jnp.arange(tok, dtype=jnp.int32)
    bounds = segment_bounds(seg_lengths, recordings)
    alive = segment_of(positions, bounds) == segment_of(positions[:1] - 1, bounds)
    entry = jnp.exp(cum) * alive.astype(f32)[None, :]
    coefs = jnp.stack(
        [
            level_weights[:, low_bits + 1 + bit, :]
            * entry
            * jnp.where(group // 2**bit % 2 == 1, befores[bit], 0.0)[:, None]
            for bit in range(high_bits)
        ]
    )

    halves = []
    for mask in range(PLACES):
        halves.append(
            list(call(
                functools.partial(far_kernel, (head_dim, recordings, state), mask),
                info,
                (sums, kq, pkq, coefs, lows[mask], pairs[mask], gate_input),
                [
                    pl.BlockSpec((tok, cols), functools.partial(quarter, recordings, mask)),
                    whole(kq.shape),
                    whole(pkq.shape),
                    whole(coefs.shape),
                    whole(lows[mask].shape),
                    whole(pairs[mask].shape),
                    pl.BlockSpec((tok, cols), functools.partial(quarter, recordings, mask)),
                ],
                [shape((tok, cols), f32), shape((tok, cols), f32)],
                [whole((tok, cols)), whole((tok, cols))],
                (1,),
                flops=4 * tok * cols * state,
            ))
        )
    queries = jnp.concatenate([pkq[:, state:], kq[HALO:, state:]], axis=0)
    tops = [all_quarters(value, bit + 2) for bit, value in enumerate(crossed)]
    for bit in range(3, high_bits):
        for mask in range(PLACES):
            first = (place ^ mask) * (cols // head_dim)
            coef = lax.dynamic_slice_in_dim(coefs[bit], first, cols // head_dim, axis=0)
            gate = lax.dynamic_slice_in_dim(gate_input, (place ^ mask) * cols, cols, axis=1)
            read = jnp.dot(queries, tops[bit - 2][mask], preferred_element_type=f32)
            read = read * jnp.repeat(coef, head_dim, axis=0).T
            halves[mask][0] = halves[mask][0] + read * jax.nn.silu(gate.astype(f32))

    rows = 64
    return call(
        functools.partial(final_kernel, (recordings, state), float(width)),
        info,
        [h[0] for h in halves] + [h[1] for h in halves] + [queries] + tops[0] + [norm_gain[None, :]],
        [pl.BlockSpec((rows, cols), lambda i, *_: (i, 0))] * (2 * PLACES)
        + [pl.BlockSpec((rows, state), lambda i, *_: (i, 0))]
        + [whole((state, cols))] * PLACES
        + [whole((1, width))],
        [shape((tok, width), bf16)],
        [pl.BlockSpec((rows, width), lambda i, *_: (i, 0))],
        (tok // rows,),
        flops=2 * tok * width * state,
    )[0]


def quarter(recordings, mask, i, info):
    return 0, jnp.bitwise_xor(lax.rem(info[recordings], PLACES), mask)


def solution(mesh):
    in_specs = (
        P(("batch", "group"), None),
        P(),
        P(),
        P(("batch", "group"), None),
        P(None, ("batch", "group")),
        P(None, None, ("batch", "group")),
        P(),
        P(),
        P("batch"),
    )
    out_specs = P(("batch", "group"), None)
    return jax.shard_map(
        per_device, mesh=mesh, in_specs=in_specs, out_specs=out_specs, check_vma=False
    )
```

```python
import functools

import jax
import jax.numpy as jnp
from jax import lax
from jax.experimental import pallas as pl
from jax.experimental.pallas import tpu as pltpu
from jax.sharding import PartitionSpec as P

eps_norm = 1e-05
bf16 = jnp.bfloat16
f32 = jnp.float32
HALO = 16
PLACES = 4
LANES = 128
EXACT = lax.Precision.HIGHEST


def iota(shape, dim):
    return lax.broadcasted_iota(jnp.int32, shape, dim)


def dot(a, b, contract, precision=None):
    return lax.dot_general(
        a, b, (contract, ((), ())), precision=precision, preferred_element_type=f32
    )


def silu(v):
    return v * (0.5 * jnp.tanh(0.5 * v) + 0.5)


def segment_bounds(lengths, recordings):
    bounds, total = [], 0
    for index in range(recordings - 1):
        total = total + lengths[index]
        bounds.append(total)
    return bounds


def segment_of(pos, bounds):
    found = jnp.where(pos >= 0, 0, -1)
    for bound in bounds:
        found = found + jnp.where(pos >= bound, 1, 0)
    return found


def same_segment(pos, other, bounds):
    return (segment_of(pos, bounds) == segment_of(other, bounds)).astype(f32)


def two_parts(value):
    high = value.astype(bf16).astype(f32)
    return high, value - high


def spread(rows, first_head, columns, head_dim):
    offset = iota((rows, LANES), 0) - iota((rows, LANES), 1) // head_dim
    tiles = []
    for tile in range(columns // LANES):
        tiles.append(
            jnp.where(offset == first_head + tile * (LANES // head_dim), 1.0, 0.0).astype(bf16)
        )
    return jnp.concatenate(tiles, axis=1)


def conv_taps(shifts, weight_ref, lo, hi):
    taps = len(shifts)
    total = weight_ref[taps : taps + 1, lo:hi]
    for tap, piece in enumerate(shifts):
        total = total + weight_ref[tap : tap + 1, lo:hi] * piece
    return silu(total)


def features_kernel(
    dims, group, x_hbm, w_hbm, b_hbm, decay_hbm, lengths_hbm,
    xs_ref, kq_ref, part_ref, cum_ref, cumt_ref, entry_ref, head_ref, weight_ref, first_ref,
    lengths, x_ref, decay_ref, shift_ref, scaled_ref, sems,
):
    tok, heads, head_dim, taps, recordings, width, state = dims
    block = 2 * state
    fetches = [
        pltpu.make_async_copy(source, target, sems.at[at])
        for at, (source, target) in enumerate(
            (
                (lengths_hbm, lengths),
                (decay_hbm, decay_ref),
                (x_hbm, x_ref),
                (w_hbm, weight_ref.at[:taps]),
                (b_hbm, weight_ref.at[taps : taps + 1]),
            )
        )
    ]
    for fetch in fetches:
        fetch.start()

    apart = iota((tok, tok), 0) - iota((tok, tok), 1)
    upper = jnp.where(apart <= 0, 1.0, 0.0)
    lower = jnp.where(apart >= 0, 1.0, 0.0)
    fetches[0].wait()
    bounds = segment_bounds(lengths, recordings)
    first = group[0] * tok
    pos = first + iota((tok, LANES), 0)
    for tap in range(1, taps):
        same = same_segment(pos, pos - tap, bounds)
        same = jnp.concatenate([same] * (tok // LANES), axis=1)
        shift_ref[(tap - 1) * tok : tap * tok] = jnp.where(apart == tap, same, 0.0).astype(bf16)
    fetches[1].wait()
    decay = jnp.concatenate(
        [decay_ref[...], jnp.zeros((LANES - heads, tok), f32)], axis=0
    )
    cum = dot(decay_ref[...], upper, ((1,), (0,)), EXACT)
    cum_ref[...] = cum
    cumt = dot(lower, decay, ((1,), (1,)), EXACT)
    cumt_ref[...] = cumt
    end = cumt[tok - 1 : tok, :]
    last = first + tok - 1
    ewt = jnp.exp(end - cumt) * same_segment(pos, last + 0 * pos, bounds)
    along = first + iota((heads, tok), 1)
    entry_ref[...] = jnp.exp(cum) * same_segment(along, first - 1 + 0 * along, bounds)
    ewt = jnp.concatenate(two_parts(ewt), axis=1).astype(bf16)
    for fetch in fetches[2:]:
        fetch.wait()

    head_ref[...] = x_ref[:HALO]
    keys = None
    for at in [width // block] + list(range(width // block)):
        lo = at * block
        rows = x_ref[:, lo : lo + block]
        moved = dot(shift_ref[...], rows, ((1,), (0,)))
        shifts = [rows.astype(f32)]
        for tap in range(1, taps):
            shifts.append(moved[(tap - 1) * tok : tap * tok])
        value = conv_taps(shifts, weight_ref, lo, lo + block)
        if keys is None:
            kq_ref[...] = value.astype(bf16)
            keys = jnp.transpose(value[:, :state])
            keys = jnp.where(iota((state, tok), 1) >= HALO, keys, 0.0).astype(bf16)
            continue
        xs = value.astype(bf16)
        xs_ref[:, lo : lo + block] = xs
        copies = spread(LANES, lo // head_dim, block, head_dim)
        weight = dot(ewt, jnp.concatenate([copies, copies], axis=0), ((1,), (0,)))
        first_ref[:, lo : lo + block] = weight[:HALO]
        scaled_ref[:, lo : lo + block] = (xs.astype(f32) * weight).astype(bf16)
    part_ref[...] = dot(keys, scaled_ref[...], ((1,), (0,)))


def join_kernel(
    dims, lengths, group, halo_ref, head_ref, w_ref, first_ref, cumt_ref, part_ref,
    px_ref, pkq_ref, own_ref, one_ref, two_ref, three_ref, scaled_ref,
):
    tok, taps, recordings, width, state = dims
    bounds = segment_bounds(lengths, recordings)
    first = group[0] * tok
    pos = first + iota((HALO, LANES), 0)
    same = [same_segment(pos, pos - tap, bounds) for tap in range(1, taps)]

    def features(lo):
        hi = lo + LANES
        both = jnp.concatenate(
            [halo_ref[:, lo:hi].astype(f32), head_ref[:, lo:hi].astype(f32)], axis=0
        )
        shifts = [both[HALO:]] + [
            pltpu.roll(both, tap, 0)[HALO:] * same[tap - 1] for tap in range(1, taps)
        ]
        return conv_taps(shifts, w_ref, lo, hi)

    keys = None
    for lo in range(width, width + 2 * state, LANES):
        part = features(lo).astype(bf16)
        pkq_ref[:, lo - width : lo - width + LANES] = part
        if lo == width:
            keys = part
    for lo in range(0, width, LANES):
        xs = features(lo).astype(bf16)
        px_ref[:, lo : lo + LANES] = xs
        scaled_ref[:, lo : lo + LANES] = (
            xs.astype(f32) * first_ref[:, lo : lo + LANES]
        ).astype(bf16)

    end = cumt_ref[tok - 1 : tok, :]
    alive = same_segment(first + tok - 1 + 0 * pos[:1], first - 1 + 0 * pos[:1], bounds)
    through = jnp.exp(end) * alive
    high, rest = two_parts(through)
    mid, low = two_parts(rest)
    row = iota((HALO, LANES), 0)
    tail = jnp.where(row == 0, high, jnp.where(row == 1, mid, jnp.where(row == 2, low, 0.0)))
    place = lax.rem(group[0], PLACES)
    cols = width // PLACES
    for mask, out_ref in ((3, three_ref), (1, one_ref), (2, two_ref), (0, own_ref)):
        where = pl.multiple_of(jnp.bitwise_xor(place, mask) * cols, LANES)
        value = part_ref[:, pl.ds(where, cols)] + dot(
            keys, scaled_ref[:, pl.ds(where, cols)], ((0,), (0,))
        )
        out_ref[:state, :] = value.astype(bf16)
        out_ref[state:, :LANES] = tail.astype(bf16)
        out_ref[state:, LANES:] = jnp.zeros((HALO, cols - LANES), bf16)


def combine_kernel(
    dims, lengths, group, own_ref, one_ref, two_ref, three_ref, quad_ref, scale_ref, weight_ref
):
    state, head_dim = dims
    cols = quad_ref.shape[1]
    place = lax.rem(group[0], PLACES)
    refs = (own_ref, one_ref, two_ref, three_ref)
    got = []
    for ref in refs:
        tail = ref[state:, :LANES].astype(f32)
        got.append(tail[0:1] + tail[1:2] + tail[2:3])
    through = []
    for at in range(PLACES):
        total = jnp.zeros((1, LANES), f32)
        for mask in range(PLACES):
            total = total + jnp.where(jnp.bitwise_xor(place, mask) == at, got[mask], 0.0)
        through.append(total)
    ones = jnp.ones((1, LANES), f32)
    rows = []
    for mask in range(PLACES):
        at = jnp.bitwise_xor(place, mask)
        product = ones
        for later in range(1, PLACES):
            product = product * jnp.where(later > at, through[later], ones)
        rows.append(product)
    for mask in range(PLACES):
        at = jnp.bitwise_xor(place, mask)
        rows.append(jnp.where(at == 0, through[1], jnp.where(at == 1, ones, 0.0 * ones)))
    before_quad = ones
    for earlier in range(PLACES - 1):
        before_quad = before_quad * jnp.where(earlier < place, through[earlier], ones)
    everything = through[0] * through[1] * through[2] * through[3]
    row = iota((8, LANES), 0)
    scale = jnp.where(row == 1, jnp.where(place == 3, through[2], ones), ones)
    scale = jnp.where(row == 2, before_quad, scale)
    scale_ref[...] = jnp.where(row == 3, everything, scale)
    weights = jnp.concatenate(rows, axis=0)
    high, low = two_parts(weights)
    copies = spread(LANES, place * (cols // head_dim), cols, head_dim)
    weights = dot(high.astype(bf16), copies, ((1,), (0,))) + dot(
        low.astype(bf16), copies, ((1,), (0,))
    )
    weight_ref[...] = weights
    for lo in range(0, cols, LANES):
        hi = lo + LANES
        quad = jnp.zeros((state, LANES), f32)
        for mask, ref in enumerate(refs):
            quad = quad + ref[:state, lo:hi].astype(f32) * weights[mask : mask + 1, lo:hi]
        quad_ref[:, lo:hi] = quad.astype(bf16)


def pair_kernel(
    dims, lengths, group, own_ref, one_ref, two_ref, three_ref, weight_ref, two_in, three_in,
    pair_ref, own_out, two_out, three_out,
):
    (state,) = dims
    cols = pair_ref.shape[1]
    for lo in range(0, cols, LANES):
        hi = lo + LANES
        pair = jnp.zeros((state, LANES), f32)
        for mask, ref in enumerate((own_ref, one_ref, two_ref, three_ref)):
            weight = weight_ref[PLACES + mask : PLACES + mask + 1, lo:hi]
            pair = pair + ref[:state, lo:hi].astype(f32) * weight
        pair_ref[:, lo:hi] = pair.astype(bf16)
    own_out[...] = own_ref[:state]
    two_out[...] = two_in[:state]
    three_out[...] = three_in[:state]


def with_head(patch, body):
    return jnp.concatenate([patch, body[HALO:]], axis=0)


def scores_kernel(dims, lengths, group, kq_ref, pkq_ref, queries_ref, scores_ref):
    tok, recordings, state = dims
    bounds = segment_bounds(lengths, recordings)
    first = group[0] * tok
    kq = with_head(pkq_ref[...], kq_ref[...])
    queries_ref[...] = kq[:, state:]
    s_pos = iota((tok, tok), 0)
    t_pos = iota((tok, tok), 1)
    valid = same_segment(first + s_pos, first + t_pos, bounds) * jnp.where(s_pos <= t_pos, 1.0, 0.0)
    scores_ref[...] = dot(kq[:, :state], kq[:, state:], ((1,), (1,))) * valid


def local_kernel(
    dims, mask, lengths, group, xs_ref, px_ref, scores_ref, cum_ref, cumt_ref, level_ref, skip_ref,
    out_ref, mixing_ref,
):
    tok, head_dim, low_bits = dims
    cols = out_ref.shape[1]
    count = cols // head_dim
    quarter = jnp.bitwise_xor(lax.rem(group[0], PLACES), mask)
    first_head = quarter * count
    rows = 32
    row_bits = rows.bit_length() - 1
    where = pl.multiple_of(quarter * cols, LANES)
    cumt = pltpu.roll(cumt_ref[...], LANES - first_head, 1)
    diff = jnp.bitwise_xor(iota((rows, tok), 0), lax.rem(iota((rows, tok), 1), rows))
    near = jnp.zeros((rows, tok), jnp.int32)
    for bit in range(row_bits):
        near = near + (diff >= 2**bit).astype(jnp.int32)
    token = iota((1, tok), 1) // rows
    lane = iota((1, 2 * head_dim), 1)
    pieces = []
    for head in range(count):
        if head % 2 == 0:
            lo = head * head_dim
            here = pl.ds(pl.multiple_of(where + lo, LANES), 2 * head_dim)
            xs = with_head(px_ref[:, here], xs_ref[:, here]).astype(f32)
            xst = jnp.transpose(xs).astype(bf16)
        cum = cum_ref[pl.ds(first_head + head, 1), :]
        levels = [level_ref[level, pl.ds(first_head + head, 1), :] for level in range(low_bits + 1)]
        inner = jnp.broadcast_to(levels[0], (rows, tok))
        for level in range(1, row_bits + 1):
            inner = jnp.where(near == level, levels[level], inner)
        for s in range(0, tok, rows):
            at = s // rows
            start = s // LANES * LANES
            outer = jnp.zeros((1, tok), f32)
            apart = jnp.bitwise_xor(token, at)
            for level in range(row_bits + 1, low_bits + 1):
                outer = jnp.where(apart >= 2 ** (level - row_bits - 1), levels[level], outer)
            picked = jnp.where(token == at, inner, outer)[:, start:]
            gap = cum[:, start:] - cumt[s : s + rows, head : head + 1]
            value = jnp.exp(jnp.minimum(gap, 0.0)) * picked
            mixing_ref[head % 2, s : s + rows, start:] = (
                value * scores_ref[s : s + rows, start:]
            ).astype(bf16)
            if start:
                mixing_ref[head % 2, s : s + rows, :start] = jnp.zeros((rows, start), bf16)
        pieces.append(
            dot(
                xst[head % 2 * head_dim : (head % 2 + 1) * head_dim],
                mixing_ref[head % 2],
                ((1,), (0,)),
            )
        )
        if head % 2 == 1:
            both = jnp.transpose(jnp.concatenate(pieces[-2:], axis=0))
            skip = jnp.where(
                lane < head_dim, skip_ref[first_head + head - 1], skip_ref[first_head + head]
            )
            out_ref[:, lo : lo + 2 * head_dim] = both + skip * xs


def spread_rows(coef, copies):
    high, low = two_parts(coef)
    return dot(high.astype(bf16), copies, ((0,), (0,))) + dot(
        low.astype(bf16), copies, ((0,), (0,))
    )


def far_kernel(
    dims, mask, lengths, group, sum_ref, queries_ref, level_ref, entry_ref, scale_ref, low_ref,
    pair_ref, gate_ref, out_ref, next_ref,
):
    head_dim, state = dims
    cols = sum_ref.shape[1]
    heads = entry_ref.shape[0]
    quarter = jnp.bitwise_xor(lax.rem(group[0], PLACES), mask)
    first = quarter * (cols // head_dim)
    queries = queries_ref[...]
    copies = spread(heads, first, cols, head_dim)
    scale = jnp.transpose(scale_ref[...])
    entry = entry_ref[...]
    factors = []
    for bit in range(3):
        on = jnp.where(lax.rem(group[0] // 2**bit, 2) == 1, 1.0, 0.0)
        coef = level_ref[bit] * entry * (scale[:heads, bit : bit + 1] * on)
        factors.append(spread_rows(coef, copies))
    total = sum_ref[...]
    for bit, ref in enumerate((low_ref, pair_ref)):
        total = total + dot(queries, ref[:state, :], ((1,), (0,))) * factors[bit]
    where = pl.multiple_of(quarter * cols, LANES)
    gate = silu(gate_ref[:, pl.ds(where, cols)].astype(f32))
    out_ref[...] = total * gate
    next_ref[...] = factors[2] * gate


def final_kernel(dims, lengths, group, *refs):
    count, rows = dims
    sums = refs[:PLACES]
    factors = refs[PLACES : 2 * PLACES]
    queries_ref = refs[2 * PLACES]
    states = refs[2 * PLACES + 1 : 3 * PLACES + 1]
    gain_ref, out_ref, gated_ref, scale_ref = refs[3 * PLACES + 1 :]
    place = lax.rem(group[0], PLACES)
    cols = sums[0].shape[1]
    step = pl.program_id(0)

    @pl.when(step == 0)
    def _():
        queries = queries_ref[...]
        squares = jnp.zeros((queries.shape[0], LANES), f32)
        for mask in range(PLACES):
            read = dot(queries, states[mask][...], ((1,), (0,)))
            value = sums[mask][...] + read * factors[mask][...]
            gated_ref[mask] = value
            for lo in range(0, cols, LANES):
                squares = squares + value[:, lo : lo + LANES] * value[:, lo : lo + LANES]
        mean = jnp.sum(squares, axis=1, keepdims=True) / count
        scale_ref[...] = jnp.broadcast_to(lax.rsqrt(mean + eps_norm), scale_ref.shape)

    here = pl.ds(pl.multiple_of(step * rows, rows), rows)
    scale = scale_ref[here, :]
    for mask in range(PLACES):
        where = pl.multiple_of(jnp.bitwise_xor(place, mask) * cols, LANES)
        for lo in range(0, cols, LANES):
            columns = pl.ds(pl.multiple_of(where + lo, LANES), LANES)
            out_ref[:, columns] = (
                gated_ref[mask, here, lo : lo + LANES] * scale * gain_ref[:, columns]
            ).astype(bf16)


VMEM = pl.BlockSpec(memory_space=pltpu.VMEM)
HBM = pl.BlockSpec(memory_space=pltpu.HBM)
SMEM = pl.BlockSpec(memory_space=pltpu.SMEM)


def call(
    kernel, scalars, operands, outs, scratch=(), flops=0, specs=None, out_specs=None, grid=(), mb=40, after=()
):
    moved = sum(a.size * a.dtype.itemsize for a in operands)
    moved += sum(o.size * o.dtype.itemsize for o in outs)
    specs = list(specs or [VMEM] * len(operands))
    first, last = len(scalars) + len(operands), len(scalars) + len(operands) + len(after)

    def body(*refs):
        kernel(*refs[:first], *refs[last:])

    return pl.pallas_call(
        body,
        grid=grid,
        in_specs=[SMEM] * len(scalars) + specs + [pl.BlockSpec(memory_space=pl.ANY)] * len(after),
        out_specs=out_specs or [VMEM] * len(outs),
        scratch_shapes=list(scratch),
        out_shape=outs,
        compiler_params=pltpu.CompilerParams(vmem_limit_bytes=mb * 2**20),
        cost_estimate=pl.CostEstimate(
            flops=flops, bytes_accessed=moved, transcendentals=0
        ),
    )(*scalars, *operands, *after)


def shape(dims, dtype):
    return jax.ShapeDtypeStruct(dims, dtype)


def per_device(
    mixed_input,
    conv_weight,
    conv_bias,
    gate_input,
    log_decay,
    level_weights,
    skip_gain,
    norm_gain,
    seg_lengths,
):
    tok, channels = mixed_input.shape
    width = gate_input.shape[1]
    heads = log_decay.shape[0]
    head_dim = width // heads
    state = (channels - width) // 2
    taps = conv_weight.shape[0]
    recordings = seg_lengths.shape[0]
    low_bits = tok.bit_length() - 1
    groups = lax.axis_size("group")
    high_bits = groups.bit_length() - 1
    group = lax.axis_index("group").astype(jnp.int32)
    place = group % PLACES
    cols = width // PLACES
    block = 2 * state
    levels = jnp.transpose(level_weights, (1, 0, 2))

    def send(value, pairs):
        return lax.ppermute(value, "group", pairs)

    def quad_send(value, mask, wanted=lambda target: True):
        pairs = [(g, g ^ mask) for g in range(groups)]
        return send(value, pairs)

    halo = send(mixed_input[tok - HALO :], [(g, g + 1) for g in range(groups - 1)])

    def in_hbm(value):
        return pltpu.with_memory_space_constraint(value, pltpu.HBM)

    xs, kq, part, cum, cumt, entry, head, weights, first, lengths = call(
        functools.partial(
            features_kernel, (tok, heads, head_dim, taps, recordings, width, state)
        ),
        (group[None],),
        (
            in_hbm(mixed_input),
            in_hbm(conv_weight),
            in_hbm(conv_bias[None, :]),
            in_hbm(log_decay),
            in_hbm(seg_lengths),
        ),
        [
            shape((tok, width), bf16),
            shape((tok, block), bf16),
            shape((state, width), f32),
            shape((heads, tok), f32),
            shape((tok, LANES), f32),
            shape((heads, tok), f32),
            shape((HALO, channels), bf16),
            shape((8, channels), f32),
            shape((HALO, width), f32),
            shape((recordings,), jnp.int32),
        ],
        [
            pltpu.VMEM((tok, channels), bf16),
            pltpu.VMEM((heads, tok), f32),
            pltpu.VMEM(((taps - 1) * tok, tok), bf16),
            pltpu.VMEM((tok, width), bf16),
            pltpu.SemaphoreType.DMA((5,)),
        ],
        flops=2 * tok * width * state,
        specs=[HBM] * 5,
        out_specs=[VMEM] * 9 + [SMEM],
    )
    scalars = (lengths, group[None])

    payload = shape((state + HALO, cols), bf16)
    px, pkq, own, one, two, three = call(
        functools.partial(join_kernel, (tok, taps, recordings, width, state)),
        scalars,
        (halo, head, weights, first, cumt, part),
        [shape((HALO, width), bf16), shape((HALO, block), bf16)] + [payload] * PLACES,
        [pltpu.VMEM((HALO, width), bf16)],
        flops=2 * HALO * width * state,
    )

    queries, scores = call(
        functools.partial(scores_kernel, (tok, recordings, state)),
        scalars,
        (kq, pkq),
        [shape((tok, state), bf16), shape((tok, tok), f32)],
        flops=2 * tok * tok * state,
    )

    def local(mask, after=()):
        return call(
            functools.partial(local_kernel, (tok, head_dim, low_bits), mask),
            scalars,
            (xs, px, scores, cum, cumt, levels[: low_bits + 1], skip_gain),
            [shape((tok, cols), f32)],
            [pltpu.VMEM((2, tok, tok), bf16)],
            specs=[VMEM] * 6 + [SMEM],
            flops=2 * cols * tok * tok,
            after=after,
        )[0]

    got_three = quad_send(three, 3)
    got_one = quad_send(one, 1)
    got_two = quad_send(two, 2)
    sums = [local(0), local(1)]
    received = (own, got_one, got_two, got_three)
    quad, scale, spread_weights = call(
        functools.partial(combine_kernel, (state, head_dim)),
        scalars,
        received,
        [shape((state, cols), bf16), shape((8, LANES), f32), shape((8, cols), f32)],
        flops=4 * state * cols,
        after=sums,
    )
    sums.append(local(2, (quad,)))
    pair, own_state, two_state, three_state = call(
        functools.partial(pair_kernel, (state,)),
        scalars,
        received + (spread_weights, two, three),
        [shape((state, cols), bf16)] * 4,
        flops=4 * state * cols,
        after=sums[2:],
    )
    sums.append(local(3, (pair,)))

    befores = [scale[0, :heads], scale[1, :heads], scale[2, :heads]]
    crossed = []
    running, total = quad, scale[3, :heads]
    for bit in range(2, high_bits):
        mask = 2**bit
        last = bit + 1 == high_bits
        far = quad_send(running, mask, lambda target: not last or target & mask)
        crossed.append(far)
        if not last:
            on_top = group // mask % 2 == 1
            far_total = quad_send(total, mask)

            def columns(value):
                mine = lax.dynamic_slice(value, (place * (cols // head_dim),), (cols // head_dim,))
                return jnp.repeat(mine, head_dim)[None, :]

            running = jnp.where(
                on_top,
                far.astype(f32) * columns(total) + running.astype(f32),
                running.astype(f32) * columns(far_total) + far.astype(f32),
            ).astype(bf16)
            befores.append(jnp.where(on_top, far_total * befores[-1], befores[-1]))
            total = total * far_total

    odd = lambda target: target & 1
    lows = [
        got_one,
        quad_send(own_state, 1, odd),
        quad_send(three_state, 1, odd),
        quad_send(two_state, 1, odd),
    ]
    pairs = [pair] + [
        quad_send(pair, mask, lambda target: target & 2) for mask in range(1, PLACES)
    ]

    def all_quarters(value, bit):
        return [value] + [
            quad_send(value, mask, lambda target: target & 2**bit)
            for mask in range(1, PLACES)
        ]

    far_levels = levels[low_bits + 1 : low_bits + 4]
    halves = [
        list(
            call(
                functools.partial(far_kernel, (head_dim, state), mask),
                scalars,
                (sums[mask], queries, far_levels, entry, scale, lows[mask], pairs[mask], gate_input),
                [shape((tok, cols), f32), shape((tok, cols), f32)],
                flops=4 * tok * cols * state,
            )
        )
        for mask in range(PLACES)
    ]
    tops = [all_quarters(value, bit + 2) for bit, value in enumerate(crossed)]
    for bit in range(3, high_bits):
        coef = levels[low_bits + 1 + bit] * entry
        coef = coef * jnp.where(group // 2**bit % 2 == 1, befores[bit], 0.0)[:, None]
        for mask in range(PLACES):
            first_head = (place ^ mask) * (cols // head_dim)
            mine = lax.dynamic_slice_in_dim(coef, first_head, cols // head_dim, axis=0)
            gate = lax.dynamic_slice_in_dim(gate_input, (place ^ mask) * cols, cols, axis=1)
            read = jnp.dot(queries, tops[bit - 2][mask], preferred_element_type=f32)
            read = read * jnp.repeat(mine, head_dim, axis=0).T
            halves[mask][0] = halves[mask][0] + read * jax.nn.silu(gate.astype(f32))

    rows = 64
    return call(
        functools.partial(final_kernel, (float(width), rows)),
        scalars,
        [h[0] for h in halves]
        + [h[1] for h in halves]
        + [queries]
        + tops[0]
        + [norm_gain[None, :]],
        [shape((tok, width), bf16)],
        [pltpu.VMEM((PLACES, tok, cols), f32), pltpu.VMEM((tok, LANES), f32)],
        out_specs=[pl.BlockSpec((rows, width), lambda i, *_: (i, 0))],
        grid=(tok // rows,),
        flops=2 * tok * width * state,
    )[0]


def solution(mesh):
    in_specs = (
        P(("batch", "group"), None),
        P(),
        P(),
        P(("batch", "group"), None),
        P(None, ("batch", "group")),
        P(None, None, ("batch", "group")),
        P(),
        P(),
        P("batch"),
    )
    out_specs = P(("batch", "group"), None)
    return jax.shard_map(
        per_device, mesh=mesh, in_specs=in_specs, out_specs=out_specs, check_vma=False
    )
```

```python
import functools

import jax
import jax.numpy as jnp
from jax import lax
from jax.experimental import pallas as pl
from jax.experimental.pallas import tpu as pltpu
from jax.sharding import PartitionSpec as P

eps_norm = 1e-05
bf16 = jnp.bfloat16
f32 = jnp.float32
HALO = 16
PLACES = 4
LANES = 128
EXACT = lax.Precision.HIGHEST


def iota(shape, dim):
    return lax.broadcasted_iota(jnp.int32, shape, dim)


def dot(a, b, contract, precision=None):
    return lax.dot_general(
        a, b, (contract, ((), ())), precision=precision, preferred_element_type=f32
    )


def silu(v):
    return v * (0.5 * jnp.tanh(0.5 * v) + 0.5)


def segment_bounds(lengths, recordings):
    bounds, total = [], 0
    for index in range(recordings - 1):
        total = total + lengths[index]
        bounds.append(total)
    return bounds


def segment_of(pos, bounds):
    found = jnp.where(pos >= 0, 0, -1)
    for bound in bounds:
        found = found + jnp.where(pos >= bound, 1, 0)
    return found


def same_segment(pos, other, bounds):
    return (segment_of(pos, bounds) == segment_of(other, bounds)).astype(f32)


def two_parts(value):
    high = value.astype(bf16).astype(f32)
    return high, value - high


def spread(rows, first_head, columns, head_dim):
    offset = iota((rows, LANES), 0) - iota((rows, LANES), 1) // head_dim
    tiles = []
    for tile in range(columns // LANES):
        tiles.append(
            jnp.where(offset == first_head + tile * (LANES // head_dim), 1.0, 0.0).astype(bf16)
        )
    return jnp.concatenate(tiles, axis=1)


def conv_taps(shifts, weight_ref, lo, hi):
    taps = len(shifts)
    total = weight_ref[taps : taps + 1, lo:hi]
    for tap, piece in enumerate(shifts):
        total = total + weight_ref[tap : tap + 1, lo:hi] * piece
    return silu(total)


def features_kernel(
    dims, group, x_hbm, w_hbm, b_hbm, decay_hbm, lengths_hbm,
    xs_ref, kq_ref, part_ref, cum_ref, cumt_ref, entry_ref, head_ref, weight_ref, first_ref,
    lengths, x_ref, decay_ref, shift_ref, scaled_ref, sems,
):
    tok, heads, head_dim, taps, recordings, width, state = dims
    block = 2 * state
    fetches = [
        pltpu.make_async_copy(source, target, sems.at[at])
        for at, (source, target) in enumerate(
            (
                (lengths_hbm, lengths),
                (decay_hbm, decay_ref),
                (x_hbm, x_ref),
                (w_hbm, weight_ref.at[:taps]),
                (b_hbm, weight_ref.at[taps]),
            )
        )
    ]
    for fetch in fetches:
        fetch.start()

    apart = iota((tok, tok), 0) - iota((tok, tok), 1)
    upper = jnp.where(apart <= 0, 1.0, 0.0)
    lower = jnp.where(apart >= 0, 1.0, 0.0)
    fetches[0].wait()
    bounds = segment_bounds(lengths, recordings)
    first = group[0] * tok
    pos = first + iota((tok, LANES), 0)
    for tap in range(1, taps):
        same = same_segment(pos, pos - tap, bounds)
        same = jnp.concatenate([same] * (tok // LANES), axis=1)
        shift_ref[(tap - 1) * tok : tap * tok] = jnp.where(apart == tap, same, 0.0).astype(bf16)
    fetches[1].wait()
    decay = jnp.concatenate(
        [decay_ref[...], jnp.zeros((LANES - heads, tok), f32)], axis=0
    )
    cum = dot(decay_ref[...], upper, ((1,), (0,)), EXACT)
    cum_ref[...] = cum
    cumt = dot(lower, decay, ((1,), (1,)), EXACT)
    cumt_ref[...] = cumt
    end = cumt[tok - 1 : tok, :]
    last = first + tok - 1
    ewt = jnp.exp(end - cumt) * same_segment(pos, last + 0 * pos, bounds)
    along = first + iota((heads, tok), 1)
    entry_ref[...] = jnp.exp(cum) * same_segment(along, first - 1 + 0 * along, bounds)
    ewt = jnp.concatenate(two_parts(ewt), axis=1).astype(bf16)
    for fetch in fetches[2:]:
        fetch.wait()

    head_ref[...] = x_ref[:HALO]
    keys = None
    for at in [width // block] + list(range(width // block)):
        lo = at * block
        rows = x_ref[:, lo : lo + block]
        moved = dot(shift_ref[...], rows, ((1,), (0,)))
        shifts = [rows.astype(f32)]
        for tap in range(1, taps):
            shifts.append(moved[(tap - 1) * tok : tap * tok])
        value = conv_taps(shifts, weight_ref, lo, lo + block)
        if keys is None:
            kq_ref[...] = value.astype(bf16)
            keys = jnp.transpose(value[:, :state])
            keys = jnp.where(iota((state, tok), 1) >= HALO, keys, 0.0).astype(bf16)
            continue
        xs = value.astype(bf16)
        xs_ref[:, lo : lo + block] = xs
        copies = spread(LANES, lo // head_dim, block, head_dim)
        weight = dot(ewt, jnp.concatenate([copies, copies], axis=0), ((1,), (0,)))
        first_ref[:, lo : lo + block] = weight[:HALO]
        scaled_ref[:, lo : lo + block] = (xs.astype(f32) * weight).astype(bf16)
    part_ref[...] = dot(keys, scaled_ref[...], ((1,), (0,)))


def join_kernel(
    dims, lengths, group, halo_ref, head_ref, w_ref, first_ref, cumt_ref, part_ref,
    px_ref, pkq_ref, own_ref, one_ref, two_ref, three_ref, scaled_ref,
):
    tok, taps, recordings, width, state = dims
    bounds = segment_bounds(lengths, recordings)
    first = group[0] * tok
    pos = first + iota((HALO, LANES), 0)
    same = [same_segment(pos, pos - tap, bounds) for tap in range(1, taps)]

    def features(lo):
        hi = lo + LANES
        both = jnp.concatenate(
            [halo_ref[:, lo:hi].astype(f32), head_ref[:, lo:hi].astype(f32)], axis=0
        )
        shifts = [both[HALO:]] + [
            pltpu.roll(both, tap, 0)[HALO:] * same[tap - 1] for tap in range(1, taps)
        ]
        return conv_taps(shifts, w_ref, lo, hi)

    keys = None
    for lo in range(width, width + 2 * state, LANES):
        part = features(lo).astype(bf16)
        pkq_ref[:, lo - width : lo - width + LANES] = part
        if lo == width:
            keys = part
    for lo in range(0, width, LANES):
        xs = features(lo).astype(bf16)
        px_ref[:, lo : lo + LANES] = xs
        scaled_ref[:, lo : lo + LANES] = (
            xs.astype(f32) * first_ref[:, lo : lo + LANES]
        ).astype(bf16)

    end = cumt_ref[tok - 1 : tok, :]
    alive = same_segment(first + tok - 1 + 0 * pos[:1], first - 1 + 0 * pos[:1], bounds)
    through = jnp.exp(end) * alive
    high, rest = two_parts(through)
    mid, low = two_parts(rest)
    row = iota((HALO, LANES), 0)
    tail = jnp.where(row == 0, high, jnp.where(row == 1, mid, jnp.where(row == 2, low, 0.0)))
    place = lax.rem(group[0], PLACES)
    cols = width // PLACES
    for mask, out_ref in ((3, three_ref), (1, one_ref), (2, two_ref), (0, own_ref)):
        where = pl.multiple_of(jnp.bitwise_xor(place, mask) * cols, LANES)
        value = part_ref[:, pl.ds(where, cols)] + dot(
            keys, scaled_ref[:, pl.ds(where, cols)], ((0,), (0,))
        )
        out_ref[:state, :] = value.astype(bf16)
        out_ref[state:, :LANES] = tail.astype(bf16)
        out_ref[state:, LANES:] = jnp.zeros((HALO, cols - LANES), bf16)


def combine_kernel(
    dims, lengths, group, own_ref, one_ref, two_ref, three_ref, quad_ref, scale_ref, weight_ref
):
    state, head_dim = dims
    cols = quad_ref.shape[1]
    place = lax.rem(group[0], PLACES)
    refs = (own_ref, one_ref, two_ref, three_ref)
    got = []
    for ref in refs:
        tail = ref[state:, :LANES].astype(f32)
        got.append(tail[0:1] + tail[1:2] + tail[2:3])
    through = []
    for at in range(PLACES):
        total = jnp.zeros((1, LANES), f32)
        for mask in range(PLACES):
            total = total + jnp.where(jnp.bitwise_xor(place, mask) == at, got[mask], 0.0)
        through.append(total)
    ones = jnp.ones((1, LANES), f32)
    rows = []
    for mask in range(PLACES):
        at = jnp.bitwise_xor(place, mask)
        product = ones
        for later in range(1, PLACES):
            product = product * jnp.where(later > at, through[later], ones)
        rows.append(product)
    for mask in range(PLACES):
        at = jnp.bitwise_xor(place, mask)
        rows.append(jnp.where(at == 0, through[1], jnp.where(at == 1, ones, 0.0 * ones)))
    before_quad = ones
    for earlier in range(PLACES - 1):
        before_quad = before_quad * jnp.where(earlier < place, through[earlier], ones)
    everything = through[0] * through[1] * through[2] * through[3]
    row = iota((8, LANES), 0)
    scale = jnp.where(row == 1, jnp.where(place == 3, through[2], ones), ones)
    scale = jnp.where(row == 2, before_quad, scale)
    scale_ref[...] = jnp.where(row == 3, everything, scale)
    weights = jnp.concatenate(rows, axis=0)
    high, low = two_parts(weights)
    copies = spread(LANES, place * (cols // head_dim), cols, head_dim)
    weights = dot(high.astype(bf16), copies, ((1,), (0,))) + dot(
        low.astype(bf16), copies, ((1,), (0,))
    )
    weight_ref[...] = weights
    for lo in range(0, cols, LANES):
        hi = lo + LANES
        quad = jnp.zeros((state, LANES), f32)
        for mask, ref in enumerate(refs):
            quad = quad + ref[:state, lo:hi].astype(f32) * weights[mask : mask + 1, lo:hi]
        quad_ref[:, lo:hi] = quad.astype(bf16)


def pair_kernel(
    dims, lengths, group, own_ref, one_ref, two_ref, three_ref, weight_ref, two_in,
    pair_ref, beside_ref, across_ref,
):
    (state,) = dims
    cols = pair_ref.shape[1]
    beside_ref[:state] = own_ref[:state]
    beside_ref[state : 2 * state] = two_in[:state]
    across_ref[state:] = three_ref[:state]
    for lo in range(0, cols, LANES):
        hi = lo + LANES
        pair = jnp.zeros((state, LANES), f32)
        for mask, ref in enumerate((own_ref, one_ref, two_ref, three_ref)):
            weight = weight_ref[PLACES + mask : PLACES + mask + 1, lo:hi]
            pair = pair + ref[:state, lo:hi].astype(f32) * weight
        pair = pair.astype(bf16)
        pair_ref[:, lo:hi] = pair
        across_ref[:state, lo:hi] = pair
        beside_ref[2 * state :, lo:hi] = pair


def with_head(patch, body):
    return jnp.concatenate([patch, body[HALO:]], axis=0)


def shared_kernel(
    dims, lengths, group, kq_ref, pkq_ref, cumt_ref, level_ref, entry_ref,
    queries_ref, scores_ref, parts_ref, coef_ref,
):
    tok, recordings, state, far_from = dims
    heads = entry_ref.shape[0]
    bounds = segment_bounds(lengths, recordings)
    first = group[0] * tok
    kq = with_head(pkq_ref[...], kq_ref[...])
    queries_ref[...] = kq[:, state:]
    s_pos = iota((tok, tok), 0)
    t_pos = iota((tok, tok), 1)
    valid = same_segment(first + s_pos, first + t_pos, bounds) * jnp.where(s_pos <= t_pos, 1.0, 0.0)
    scores_ref[...] = dot(kq[:, :state], kq[:, state:], ((1,), (1,))) * valid
    high, rest = two_parts(cumt_ref[...])
    mid, low = two_parts(rest)
    parts_ref[...] = jnp.concatenate([high, mid, low], axis=1).astype(bf16)
    for bit in range(coef_ref.shape[0]):
        coef = level_ref[far_from + bit] * entry_ref[...]
        coef = jnp.concatenate([coef, jnp.zeros((LANES - heads, tok), f32)], axis=0)
        coef_ref[bit] = jnp.transpose(coef)


def local_kernel(
    dims, mask, lengths, group, xs_ref, px_ref, scores_ref, cum_ref, parts_ref, level_ref, skip_ref,
    out_ref, mixing_ref, copied_ref,
):
    tok, head_dim, low_bits = dims
    cols = out_ref.shape[1]
    count = cols // head_dim
    quarter = jnp.bitwise_xor(lax.rem(group[0], PLACES), mask)
    first_head = quarter * count
    rows = 32
    row_bits = rows.bit_length() - 1
    where = pl.multiple_of(quarter * cols, LANES)
    copies = spread(LANES, first_head, count * LANES, LANES)
    copied_ref[...] = dot(parts_ref[...], jnp.concatenate([copies] * 3, axis=0), ((1,), (0,)))
    diff = jnp.bitwise_xor(iota((rows, tok), 0), lax.rem(iota((rows, tok), 1), rows))
    near = jnp.zeros((rows, tok), jnp.int32)
    for bit in range(row_bits):
        near = near + (diff >= 2**bit).astype(jnp.int32)
    token = iota((1, tok), 1) // rows
    lane = iota((1, 2 * head_dim), 1)
    unit = jnp.where(iota((tok, tok), 0) == iota((tok, tok), 1), 1.0, 0.0).astype(bf16)
    mixing_ref[...] = jnp.zeros(mixing_ref.shape, bf16)
    pieces = []
    for head in range(count):
        if head % 2 == 0:
            lo = head * head_dim
            here = pl.ds(pl.multiple_of(where + lo, LANES), 2 * head_dim)
            xs = with_head(px_ref[:, here], xs_ref[:, here])
            xst = jnp.transpose(xs)
        cum = cum_ref[pl.ds(first_head + head, 1), :]
        levels = [level_ref[level, pl.ds(first_head + head, 1), :] for level in range(low_bits + 1)]
        inner = jnp.broadcast_to(levels[0], (rows, tok))
        for level in range(1, row_bits + 1):
            inner = jnp.where(near == level, levels[level], inner)
        for s in range(0, tok, rows):
            at = s // rows
            outer = jnp.zeros((1, tok), f32)
            apart = jnp.bitwise_xor(token, at)
            for level in range(row_bits + 1, low_bits + 1):
                outer = jnp.where(apart >= 2 ** (level - row_bits - 1), levels[level], outer)
            before = copied_ref[s : s + rows, head * LANES : (head + 1) * LANES]
            for t in range(s // LANES * LANES, tok, LANES):
                here_t = slice(t, t + LANES)
                picked = outer[:, here_t]
                gap = cum[:, here_t] - before
                if t <= s:
                    picked = jnp.where(token[:, here_t] == at, inner[:, here_t], picked)
                    gap = jnp.minimum(gap, 0.0)
                mixing_ref[head % 2, s : s + rows, here_t] = (
                    jnp.exp(gap) * picked * scores_ref[s : s + rows, here_t]
                ).astype(bf16)
        pieces.append(
            dot(
                xst[head % 2 * head_dim : (head % 2 + 1) * head_dim],
                mixing_ref[head % 2],
                ((1,), (0,)),
            )
        )
        if head % 2 == 1:
            both = jnp.concatenate(pieces[-2:], axis=0)
            skip = jnp.where(
                lane < head_dim, skip_ref[first_head + head - 1], skip_ref[first_head + head]
            )
            out_ref[:, lo : lo + 2 * head_dim] = jnp.transpose(both) + skip * xs.astype(f32)


def far_kernel(
    dims, mask, lengths, group, sum_ref, queries_ref, coef_ref, scale_ref, low_ref,
    pair_ref, gate_ref, out_ref, next_ref,
):
    head_dim, state, low_from, pair_from = dims
    tok, cols = sum_ref.shape
    quarter = jnp.bitwise_xor(lax.rem(group[0], PLACES), mask)
    first = quarter * (cols // head_dim)
    queries = queries_ref[...]
    coefs = []
    for bit in range(coef_ref.shape[0]):
        on = jnp.where(lax.rem(group[0] // 2**bit, 2) == 1, 1.0, 0.0)
        coef = two_parts(coef_ref[bit] * (scale_ref[bit : bit + 1, :] * on))
        coefs.append(jnp.concatenate(coef, axis=1).astype(bf16))
    copies = spread(LANES, first, cols, head_dim)
    factors = dot(
        jnp.concatenate(coefs, axis=0), jnp.concatenate([copies, copies], axis=0), ((1,), (0,))
    )
    total = sum_ref[...]
    for bit, state_in in enumerate(
        (low_ref[low_from : low_from + state], pair_ref[pair_from : pair_from + state])
    ):
        total = total + dot(queries, state_in, ((1,), (0,))) * factors[bit * tok : (bit + 1) * tok]
    where = pl.multiple_of(quarter * cols, LANES)
    gate = silu(gate_ref[:, pl.ds(where, cols)].astype(f32))
    out_ref[...] = total * gate
    next_ref[...] = factors[2 * tok :] * gate


def final_kernel(dims, lengths, group, *refs):
    count, rows = dims
    sums = refs[:PLACES]
    factors = refs[PLACES : 2 * PLACES]
    queries_ref = refs[2 * PLACES]
    states = refs[2 * PLACES + 1 : 3 * PLACES + 1]
    gain_ref, out_ref, gated_ref, scale_ref = refs[3 * PLACES + 1 :]
    place = lax.rem(group[0], PLACES)
    cols = sums[0].shape[1]
    step = pl.program_id(0)

    @pl.when(step == 0)
    def _():
        queries = queries_ref[...]
        squares = jnp.zeros((queries.shape[0], LANES), f32)
        for mask in range(PLACES):
            read = dot(queries, states[mask][...], ((1,), (0,)))
            value = sums[mask][...] + read * factors[mask][...]
            gated_ref[mask] = value
            for lo in range(0, cols, LANES):
                squares = squares + value[:, lo : lo + LANES] * value[:, lo : lo + LANES]
        mean = jnp.sum(squares, axis=1, keepdims=True) / count
        scale_ref[...] = jnp.broadcast_to(lax.rsqrt(mean + eps_norm), scale_ref.shape)

    here = pl.ds(pl.multiple_of(step * rows, rows), rows)
    scale = scale_ref[here, :]
    for mask in range(PLACES):
        where = pl.multiple_of(jnp.bitwise_xor(place, mask) * cols, LANES)
        for lo in range(0, cols, LANES):
            columns = pl.ds(pl.multiple_of(where + lo, LANES), LANES)
            out_ref[:, columns] = (
                gated_ref[mask, here, lo : lo + LANES] * scale * gain_ref[:, columns]
            ).astype(bf16)


VMEM = pl.BlockSpec(memory_space=pltpu.VMEM)
HBM = pl.BlockSpec(memory_space=pltpu.HBM)
SMEM = pl.BlockSpec(memory_space=pltpu.SMEM)


def call(
    kernel, scalars, operands, outs, scratch=(), flops=0, specs=None, out_specs=None, grid=(), mb=40, after=()
):
    moved = sum(a.size * a.dtype.itemsize for a in operands)
    moved += sum(o.size * o.dtype.itemsize for o in outs)
    specs = list(specs or [VMEM] * len(operands))
    first, last = len(scalars) + len(operands), len(scalars) + len(operands) + len(after)

    def body(*refs):
        kernel(*refs[:first], *refs[last:])

    return pl.pallas_call(
        body,
        grid=grid,
        in_specs=[SMEM] * len(scalars) + specs + [pl.BlockSpec(memory_space=pl.ANY)] * len(after),
        out_specs=out_specs or [VMEM] * len(outs),
        scratch_shapes=list(scratch),
        out_shape=outs,
        compiler_params=pltpu.CompilerParams(vmem_limit_bytes=mb * 2**20),
        cost_estimate=pl.CostEstimate(
            flops=flops, bytes_accessed=moved, transcendentals=0
        ),
    )(*scalars, *operands, *after)


def shape(dims, dtype):
    return jax.ShapeDtypeStruct(dims, dtype)


def per_device(
    mixed_input,
    conv_weight,
    conv_bias,
    gate_input,
    log_decay,
    level_weights,
    skip_gain,
    norm_gain,
    seg_lengths,
):
    tok, channels = mixed_input.shape
    width = gate_input.shape[1]
    heads = log_decay.shape[0]
    head_dim = width // heads
    state = (channels - width) // 2
    taps = conv_weight.shape[0]
    recordings = seg_lengths.shape[0]
    low_bits = tok.bit_length() - 1
    groups = lax.axis_size("group")
    high_bits = groups.bit_length() - 1
    group = lax.axis_index("group").astype(jnp.int32)
    place = group % PLACES
    cols = width // PLACES
    block = 2 * state
    levels = jnp.transpose(level_weights, (1, 0, 2))

    def send(value, pairs):
        return lax.ppermute(value, "group", pairs)

    def quad_send(value, mask, wanted=lambda source, target: True):
        pairs = [(g, g ^ mask) for g in range(groups) if wanted(g, g ^ mask)]
        return send(value, pairs)

    halo = send(mixed_input[tok - HALO :], [(g, g + 1) for g in range(groups - 1)])

    def in_hbm(value):
        return pltpu.with_memory_space_constraint(value, pltpu.HBM)

    xs, kq, part, cum, cumt, entry, head, weights, first, lengths = call(
        functools.partial(
            features_kernel, (tok, heads, head_dim, taps, recordings, width, state)
        ),
        (group[None],),
        (
            in_hbm(mixed_input),
            in_hbm(conv_weight),
            in_hbm(conv_bias),
            in_hbm(log_decay),
            in_hbm(seg_lengths),
        ),
        [
            shape((tok, width), bf16),
            shape((tok, block), bf16),
            shape((state, width), f32),
            shape((heads, tok), f32),
            shape((tok, LANES), f32),
            shape((heads, tok), f32),
            shape((HALO, channels), bf16),
            shape((8, channels), f32),
            shape((HALO, width), f32),
            shape((recordings,), jnp.int32),
        ],
        [
            pltpu.VMEM((tok, channels), bf16),
            pltpu.VMEM((heads, tok), f32),
            pltpu.VMEM(((taps - 1) * tok, tok), bf16),
            pltpu.VMEM((tok, width), bf16),
            pltpu.SemaphoreType.DMA((5,)),
        ],
        flops=2 * tok * width * state,
        specs=[HBM] * 5,
        out_specs=[VMEM] * 9 + [SMEM],
    )
    scalars = (lengths, group[None])

    payload = shape((state + HALO, cols), bf16)
    px, pkq, own, one, two, three = call(
        functools.partial(join_kernel, (tok, taps, recordings, width, state)),
        scalars,
        (halo, head, weights, first, cumt, part),
        [shape((HALO, width), bf16), shape((HALO, block), bf16)] + [payload] * PLACES,
        [pltpu.VMEM((HALO, width), bf16)],
        flops=2 * HALO * width * state,
    )

    queries, scores, parts, coefs = call(
        functools.partial(shared_kernel, (tok, recordings, state, low_bits + 1)),
        scalars,
        (kq, pkq, cumt, levels, entry),
        [
            shape((tok, state), bf16),
            shape((tok, tok), f32),
            shape((tok, 3 * LANES), bf16),
            shape((3, tok, LANES), f32),
        ],
        flops=2 * tok * tok * state,
    )

    def local(mask, after=()):
        return call(
            functools.partial(local_kernel, (tok, head_dim, low_bits), mask),
            scalars,
            (xs, px, scores, cum, parts, levels, skip_gain),
            [shape((tok, cols), f32)],
            [pltpu.VMEM((2, tok, tok), bf16), pltpu.VMEM((tok, cols // head_dim * LANES), f32)],
            specs=[VMEM] * 6 + [SMEM],
            flops=2 * cols * tok * tok,
            after=after,
        )[0]

    got_three = quad_send(three, 3)
    got_one = quad_send(one, 1)
    got_two = quad_send(two, 2)
    sums = [local(0), local(1)]
    received = (own, got_one, got_two, got_three)
    quad, scale, spread_weights = call(
        functools.partial(combine_kernel, (state, head_dim)),
        scalars,
        received,
        [shape((state, cols), bf16), shape((8, LANES), f32), shape((8, cols), f32)],
        flops=4 * state * cols,
        after=sums,
    )
    pair, beside, across = call(
        functools.partial(pair_kernel, (state,)),
        scalars,
        received + (spread_weights, two),
        [
            shape((state, cols), bf16),
            shape((3 * state, cols), bf16),
            shape((2 * state, cols), bf16),
        ],
        flops=4 * state * cols,
        after=(quad,),
    )
    sums.append(local(2, (quad,)))
    sums.append(local(3, ()))
    got_three_of_pair = quad_send(pair, 3, lambda source, target: target & 2)
    got_beside = quad_send(beside, 1)
    got_across = quad_send(across, 2)

    befores = [scale[0, :heads], scale[1, :heads], scale[2, :heads]]
    crossed = []
    running, total = quad, scale[3, :heads]
    for bit in range(2, high_bits):
        mask = 2**bit
        last = bit + 1 == high_bits
        far = quad_send(running, mask, lambda source, target: True)
        crossed.append(lax.optimization_barrier((far, sums[3], sums[2]))[0])
        if not last:
            on_top = group // mask % 2 == 1
            far_total = quad_send(total, mask)

            def columns(value):
                mine = lax.dynamic_slice(value, (place * (cols // head_dim),), (cols // head_dim,))
                return jnp.repeat(mine, head_dim)[None, :]

            running = jnp.where(
                on_top,
                far.astype(f32) * columns(total) + running.astype(f32),
                running.astype(f32) * columns(far_total) + far.astype(f32),
            ).astype(bf16)
            befores.append(jnp.where(on_top, far_total * befores[-1], befores[-1]))
            total = total * far_total

    lows = [(got_one, 0), (got_beside, 0), (got_across, state), (got_beside, state)]
    pairs = [(pair, 0), (got_beside, 2 * state), (got_across, 0), (got_three_of_pair, 0)]

    def all_quarters(value, bit):
        return [value] + [
            quad_send(value, mask)
            for mask in range(1, PLACES)
        ]

    halves = [
        list(
            call(
                functools.partial(far_kernel, (head_dim, state, lows[mask][1], pairs[mask][1]), mask),
                scalars,
                (sums[mask], queries, coefs, scale, lows[mask][0], pairs[mask][0], gate_input),
                [shape((tok, cols), f32), shape((tok, cols), f32)],
                flops=4 * tok * cols * state,
            )
        )
        for mask in range(PLACES)
    ]
    tops = [all_quarters(value, bit + 2) for bit, value in enumerate(crossed)]
    for bit in range(3, high_bits):
        coef = levels[low_bits + 1 + bit] * entry
        coef = coef * jnp.where(group // 2**bit % 2 == 1, befores[bit], 0.0)[:, None]
        for mask in range(PLACES):
            first_head = (place ^ mask) * (cols // head_dim)
            mine = lax.dynamic_slice_in_dim(coef, first_head, cols // head_dim, axis=0)
            gate = lax.dynamic_slice_in_dim(gate_input, (place ^ mask) * cols, cols, axis=1)
            read = jnp.dot(queries, tops[bit - 2][mask], preferred_element_type=f32)
            read = read * jnp.repeat(mine, head_dim, axis=0).T
            halves[mask][0] = halves[mask][0] + read * jax.nn.silu(gate.astype(f32))

    rows = 128
    return call(
        functools.partial(final_kernel, (float(width), rows)),
        scalars,
        [h[0] for h in halves]
        + [h[1] for h in halves]
        + [queries]
        + tops[0]
        + [norm_gain[None, :]],
        [shape((tok, width), bf16)],
        [pltpu.VMEM((PLACES, tok, cols), f32), pltpu.VMEM((tok, LANES), f32)],
        out_specs=[pl.BlockSpec((rows, width), lambda i, *_: (i, 0))],
        grid=(tok // rows,),
        flops=2 * tok * width * state,
    )[0]


def solution(mesh):
    in_specs = (
        P(("batch", "group"), None),
        P(),
        P(),
        P(("batch", "group"), None),
        P(None, ("batch", "group")),
        P(None, None, ("batch", "group")),
        P(),
        P(),
        P("batch"),
    )
    out_specs = P(("batch", "group"), None)
    return jax.shard_map(
        per_device, mesh=mesh, in_specs=in_specs, out_specs=out_specs, check_vma=False
    )
```

```python
import functools

import jax
import jax.numpy as jnp
from jax import lax
from jax.experimental import pallas as pl
from jax.experimental.pallas import tpu as pltpu
from jax.sharding import PartitionSpec as P

eps_norm = 1e-05
bf16 = jnp.bfloat16
f32 = jnp.float32
HALO = 16
PLACES = 4
LANES = 128


def iota(shape, dim):
    return lax.broadcasted_iota(jnp.int32, shape, dim)


def dot(a, b, contract, precision=None):
    return lax.dot_general(
        a, b, (contract, ((), ())), precision=precision, preferred_element_type=f32
    )


def silu(v):
    return v * (0.5 * jnp.tanh(0.5 * v) + 0.5)


def segment_bounds(lengths, recordings):
    bounds, total = [], 0
    for index in range(recordings - 1):
        total = total + lengths[index]
        bounds.append(total)
    return bounds


def segment_of(pos, bounds):
    found = jnp.where(pos >= 0, 0, -1)
    for bound in bounds:
        found = found + jnp.where(pos >= bound, 1, 0)
    return found


def same_segment(pos, other, bounds):
    return (segment_of(pos, bounds) == segment_of(other, bounds)).astype(f32)


def two_parts(value):
    high = value.astype(bf16).astype(f32)
    return high, value - high


def spread(rows, first_head, columns, head_dim):
    offset = iota((rows, LANES), 0) - iota((rows, LANES), 1) // head_dim
    tiles = []
    for tile in range(columns // LANES):
        tiles.append(
            jnp.where(offset == first_head + tile * (LANES // head_dim), 1.0, 0.0).astype(bf16)
        )
    return jnp.concatenate(tiles, axis=1)


def conv_taps(shifts, weight_ref, lo, hi):
    taps = len(shifts)
    total = weight_ref[taps : taps + 1, lo:hi]
    for tap, piece in enumerate(shifts):
        total = total + weight_ref[tap : tap + 1, lo:hi] * piece
    return silu(total)


def features_kernel(
    dims, group, x_hbm, w_hbm, b_hbm, decay_hbm, lengths_hbm,
    xs_ref, kq_ref, part_ref, cum_ref, cumt_ref, entry_ref, head_ref, weight_ref, first_ref,
    lengths, x_ref, decay_ref, shift_ref, scaled_ref, sems,
):
    tok, heads, head_dim, taps, recordings, width, state = dims
    block = 2 * state
    fetches = [
        pltpu.make_async_copy(source, target, sems.at[at])
        for at, (source, target) in enumerate(
            (
                (lengths_hbm, lengths),
                (decay_hbm, decay_ref),
                (x_hbm, x_ref),
                (w_hbm, weight_ref.at[:taps]),
                (b_hbm, weight_ref.at[taps]),
            )
        )
    ]
    for fetch in fetches:
        fetch.start()

    apart = iota((tok, tok), 0) - iota((tok, tok), 1)
    upper = jnp.where(apart <= 0, 1.0, 0.0).astype(bf16)
    lower = jnp.where(apart >= 0, 1.0, 0.0).astype(bf16)
    fetches[0].wait()
    bounds = segment_bounds(lengths, recordings)
    first = group[0] * tok
    pos = first + iota((tok, LANES), 0)
    for tap in range(1, taps):
        same = same_segment(pos, pos - tap, bounds)
        same = jnp.concatenate([same] * (tok // LANES), axis=1)
        shift_ref[(tap - 1) * tok : tap * tok] = jnp.where(apart == tap, same, 0.0).astype(bf16)
    fetches[1].wait()
    pad = jnp.zeros((LANES - heads, tok), f32)
    high, rest = two_parts(jnp.concatenate([decay_ref[...], pad], axis=0))
    mid, low = two_parts(rest)
    parts = jnp.concatenate([high, mid, low], axis=0).astype(bf16)
    cum = dot(parts, upper, ((1,), (0,)))
    cum = cum[:heads] + cum[LANES : LANES + heads] + cum[2 * LANES : 2 * LANES + heads]
    cum_ref[...] = cum
    cumt = dot(lower, parts, ((1,), (1,)))
    cumt = cumt[:, :LANES] + cumt[:, LANES : 2 * LANES] + cumt[:, 2 * LANES :]
    cumt_ref[...] = cumt
    end = cumt[tok - 1 : tok, :]
    last = first + tok - 1
    ewt = jnp.exp(end - cumt) * same_segment(pos, last + 0 * pos, bounds)
    along = first + iota((heads, tok), 1)
    entry_ref[...] = jnp.exp(cum) * same_segment(along, first - 1 + 0 * along, bounds)
    ewt = jnp.concatenate(two_parts(ewt), axis=1).astype(bf16)
    for fetch in fetches[2:]:
        fetch.wait()

    head_ref[...] = x_ref[:HALO]
    keys = None
    for at in [width // block] + list(range(width // block)):
        lo = at * block
        rows = x_ref[:, lo : lo + block]
        moved = dot(shift_ref[...], rows, ((1,), (0,)))
        shifts = [rows.astype(f32)]
        for tap in range(1, taps):
            shifts.append(moved[(tap - 1) * tok : tap * tok])
        value = conv_taps(shifts, weight_ref, lo, lo + block)
        if keys is None:
            kq_ref[...] = value.astype(bf16)
            keys = jnp.transpose(value[:, :state])
            keys = jnp.where(iota((state, tok), 1) >= HALO, keys, 0.0).astype(bf16)
            continue
        xs = value.astype(bf16)
        xs_ref[:, lo : lo + block] = xs
        copies = spread(LANES, lo // head_dim, block, head_dim)
        weight = dot(ewt, jnp.concatenate([copies, copies], axis=0), ((1,), (0,)))
        first_ref[:, lo : lo + block] = weight[:HALO]
        scaled_ref[:, lo : lo + block] = (xs.astype(f32) * weight).astype(bf16)
    part_ref[...] = dot(keys, scaled_ref[...], ((1,), (0,)))


def join_kernel(
    dims, lengths, group, halo_ref, head_ref, w_ref, first_ref, cumt_ref, part_ref,
    px_ref, pkq_ref, own_ref, one_ref, two_ref, three_ref, scaled_ref,
):
    tok, taps, recordings, width, state = dims
    bounds = segment_bounds(lengths, recordings)
    first = group[0] * tok
    pos = first + iota((HALO, LANES), 0)
    same = [same_segment(pos, pos - tap, bounds) for tap in range(1, taps)]

    def features(lo):
        hi = lo + LANES
        both = jnp.concatenate(
            [halo_ref[:, lo:hi].astype(f32), head_ref[:, lo:hi].astype(f32)], axis=0
        )
        shifts = [both[HALO:]] + [
            pltpu.roll(both, tap, 0)[HALO:] * same[tap - 1] for tap in range(1, taps)
        ]
        return conv_taps(shifts, w_ref, lo, hi)

    keys = None
    for lo in range(width, width + 2 * state, LANES):
        part = features(lo).astype(bf16)
        pkq_ref[:, lo - width : lo - width + LANES] = part
        if lo == width:
            keys = part
    for lo in range(0, width, LANES):
        xs = features(lo).astype(bf16)
        px_ref[:, lo : lo + LANES] = xs
        scaled_ref[:, lo : lo + LANES] = (
            xs.astype(f32) * first_ref[:, lo : lo + LANES]
        ).astype(bf16)

    end = cumt_ref[tok - 1 : tok, :]
    alive = same_segment(first + tok - 1 + 0 * pos[:1], first - 1 + 0 * pos[:1], bounds)
    through = jnp.exp(end) * alive
    high, rest = two_parts(through)
    mid, low = two_parts(rest)
    row = iota((HALO, LANES), 0)
    tail = jnp.where(row == 0, high, jnp.where(row == 1, mid, jnp.where(row == 2, low, 0.0)))
    place = lax.rem(group[0], PLACES)
    cols = width // PLACES
    for mask, out_ref in ((3, three_ref), (1, one_ref), (2, two_ref), (0, own_ref)):
        where = pl.multiple_of(jnp.bitwise_xor(place, mask) * cols, LANES)
        value = part_ref[:, pl.ds(where, cols)] + dot(
            keys, scaled_ref[:, pl.ds(where, cols)], ((0,), (0,))
        )
        out_ref[:state, :] = value.astype(bf16)
        out_ref[state:, :LANES] = tail.astype(bf16)
        out_ref[state:, LANES:] = jnp.zeros((HALO, cols - LANES), bf16)


def combine_kernel(
    dims, lengths, group, own_ref, one_ref, two_ref, three_ref, quad_ref, scale_ref, weight_ref
):
    state, head_dim = dims
    cols = quad_ref.shape[1]
    place = lax.rem(group[0], PLACES)
    refs = (own_ref, one_ref, two_ref, three_ref)
    got = []
    for ref in refs:
        tail = ref[state:, :LANES].astype(f32)
        got.append(tail[0:1] + tail[1:2] + tail[2:3])
    through = []
    for at in range(PLACES):
        total = jnp.zeros((1, LANES), f32)
        for mask in range(PLACES):
            total = total + jnp.where(jnp.bitwise_xor(place, mask) == at, got[mask], 0.0)
        through.append(total)
    ones = jnp.ones((1, LANES), f32)
    rows = []
    for mask in range(PLACES):
        at = jnp.bitwise_xor(place, mask)
        product = ones
        for later in range(1, PLACES):
            product = product * jnp.where(later > at, through[later], ones)
        rows.append(product)
    for mask in range(PLACES):
        at = jnp.bitwise_xor(place, mask)
        rows.append(jnp.where(at == 0, through[1], jnp.where(at == 1, ones, 0.0 * ones)))
    before_quad = ones
    for earlier in range(PLACES - 1):
        before_quad = before_quad * jnp.where(earlier < place, through[earlier], ones)
    everything = through[0] * through[1] * through[2] * through[3]
    row = iota((8, LANES), 0)
    scale = jnp.where(row == 1, jnp.where(place == 3, through[2], ones), ones)
    scale = jnp.where(row == 2, before_quad, scale)
    scale_ref[...] = jnp.where(row == 3, everything, scale)
    weights = jnp.concatenate(rows, axis=0)
    high, low = two_parts(weights)
    copies = spread(LANES, place * (cols // head_dim), cols, head_dim)
    weights = dot(high.astype(bf16), copies, ((1,), (0,))) + dot(
        low.astype(bf16), copies, ((1,), (0,))
    )
    weight_ref[...] = weights
    for lo in range(0, cols, LANES):
        hi = lo + LANES
        quad = jnp.zeros((state, LANES), f32)
        for mask, ref in enumerate(refs):
            quad = quad + ref[:state, lo:hi].astype(f32) * weights[mask : mask + 1, lo:hi]
        quad_ref[:, lo:hi] = quad.astype(bf16)


def pair_kernel(
    dims, lengths, group, own_ref, one_ref, two_ref, three_ref, weight_ref, two_in,
    pair_ref, beside_ref, across_ref,
):
    (state,) = dims
    cols = pair_ref.shape[1]
    beside_ref[:state] = own_ref[:state]
    beside_ref[state : 2 * state] = two_in[:state]
    across_ref[state:] = three_ref[:state]
    for lo in range(0, cols, LANES):
        hi = lo + LANES
        pair = jnp.zeros((state, LANES), f32)
        for mask, ref in enumerate((own_ref, one_ref, two_ref, three_ref)):
            weight = weight_ref[PLACES + mask : PLACES + mask + 1, lo:hi]
            pair = pair + ref[:state, lo:hi].astype(f32) * weight
        pair = pair.astype(bf16)
        pair_ref[:, lo:hi] = pair
        across_ref[:state, lo:hi] = pair
        beside_ref[2 * state :, lo:hi] = pair


def with_head(patch, body):
    return jnp.concatenate([patch, body[HALO:]], axis=0)


def shared_kernel(
    dims, lengths, group, kq_ref, pkq_ref, cumt_ref, level_ref, entry_ref,
    queries_ref, scores_ref, parts_ref, coef_ref,
):
    tok, recordings, state, far_from = dims
    heads = entry_ref.shape[0]
    bounds = segment_bounds(lengths, recordings)
    first = group[0] * tok
    kq = with_head(pkq_ref[...], kq_ref[...])
    queries_ref[...] = kq[:, state:]
    s_pos = iota((tok, tok), 0)
    t_pos = iota((tok, tok), 1)
    valid = same_segment(first + s_pos, first + t_pos, bounds) * jnp.where(s_pos <= t_pos, 1.0, 0.0)
    scores_ref[...] = dot(kq[:, :state], kq[:, state:], ((1,), (1,))) * valid
    high, rest = two_parts(cumt_ref[...])
    mid, low = two_parts(rest)
    parts_ref[...] = jnp.concatenate([high, mid, low], axis=1).astype(bf16)
    for bit in range(coef_ref.shape[0]):
        coef = level_ref[far_from + bit] * entry_ref[...]
        coef = jnp.concatenate([coef, jnp.zeros((LANES - heads, tok), f32)], axis=0)
        coef_ref[bit] = jnp.transpose(coef)


def local_kernel(
    dims, mask, lengths, group, xs_ref, px_ref, scores_ref, cum_ref, parts_ref, level_ref, skip_ref,
    out_ref, mixing_ref, copied_ref,
):
    tok, head_dim, low_bits = dims
    cols = out_ref.shape[1]
    count = cols // head_dim
    quarter = jnp.bitwise_xor(lax.rem(group[0], PLACES), mask)
    first_head = quarter * count
    rows = 32
    row_bits = rows.bit_length() - 1
    where = pl.multiple_of(quarter * cols, LANES)
    copies = spread(LANES, first_head, count * LANES, LANES)
    copied_ref[...] = dot(parts_ref[...], jnp.concatenate([copies] * 3, axis=0), ((1,), (0,)))
    diff = jnp.bitwise_xor(iota((rows, tok), 0), lax.rem(iota((rows, tok), 1), rows))
    near = jnp.zeros((rows, tok), jnp.int32)
    for bit in range(row_bits):
        near = near + (diff >= 2**bit).astype(jnp.int32)
    token = iota((1, tok), 1) // rows
    lane = iota((1, 2 * head_dim), 1)
    unit = jnp.where(iota((tok, tok), 0) == iota((tok, tok), 1), 1.0, 0.0).astype(bf16)
    mixing_ref[...] = jnp.zeros(mixing_ref.shape, bf16)
    pieces = []
    for head in range(count):
        if head % 2 == 0:
            lo = head * head_dim
            here = pl.ds(pl.multiple_of(where + lo, LANES), 2 * head_dim)
            xs = with_head(px_ref[:, here], xs_ref[:, here])
            xst = jnp.transpose(xs)
        cum = cum_ref[pl.ds(first_head + head, 1), :]
        levels = [level_ref[level, pl.ds(first_head + head, 1), :] for level in range(low_bits + 1)]
        inner = jnp.broadcast_to(levels[0], (rows, tok))
        for level in range(1, row_bits + 1):
            inner = jnp.where(near == level, levels[level], inner)
        for s in range(0, tok, rows):
            at = s // rows
            outer = jnp.zeros((1, tok), f32)
            apart = jnp.bitwise_xor(token, at)
            for level in range(row_bits + 1, low_bits + 1):
                outer = jnp.where(apart >= 2 ** (level - row_bits - 1), levels[level], outer)
            before = copied_ref[s : s + rows, head * LANES : (head + 1) * LANES]
            for t in range(s // LANES * LANES, tok, LANES):
                here_t = slice(t, t + LANES)
                picked = outer[:, here_t]
                gap = cum[:, here_t] - before
                if t <= s:
                    picked = jnp.where(token[:, here_t] == at, inner[:, here_t], picked)
                    gap = jnp.minimum(gap, 0.0)
                mixing_ref[head % 2, s : s + rows, here_t] = (
                    jnp.exp(gap) * picked * scores_ref[s : s + rows, here_t]
                ).astype(bf16)
        pieces.append(
            dot(
                xst[head % 2 * head_dim : (head % 2 + 1) * head_dim],
                mixing_ref[head % 2],
                ((1,), (0,)),
            )
        )
        if head % 2 == 1:
            both = jnp.concatenate(pieces[-2:], axis=0)
            skip = jnp.where(
                lane < head_dim, skip_ref[first_head + head - 1], skip_ref[first_head + head]
            )
            out_ref[:, lo : lo + 2 * head_dim] = jnp.transpose(both) + skip * xs.astype(f32)


def far_kernel(
    dims, mask, lengths, group, sum_ref, queries_ref, coef_ref, scale_ref, low_ref,
    pair_ref, gate_ref, *refs,
):
    head_dim, state, low_from, pair_from = dims
    tok, cols = sum_ref.shape
    quarter = jnp.bitwise_xor(lax.rem(group[0], PLACES), mask)
    first = quarter * (cols // head_dim)
    queries = queries_ref[...]
    coefs = []
    for bit in range(coef_ref.shape[0]):
        on = jnp.where(lax.rem(group[0] // 2**bit, 2) == 1, 1.0, 0.0)
        coef = two_parts(coef_ref[bit] * (scale_ref[bit : bit + 1, :] * on))
        coefs.append(jnp.concatenate(coef, axis=1).astype(bf16))
    copies = spread(LANES, first, cols, head_dim)
    factors = dot(
        jnp.concatenate(coefs, axis=0), jnp.concatenate([copies, copies], axis=0), ((1,), (0,))
    )
    total = sum_ref[...]
    states = [low_ref[low_from : low_from + state], pair_ref[pair_from : pair_from + state]]
    if len(refs) > 2:
        states.append(refs[0][...])
    for bit, state_in in enumerate(states):
        total = total + dot(queries, state_in, ((1,), (0,))) * factors[bit * tok : (bit + 1) * tok]
    where = pl.multiple_of(quarter * cols, LANES)
    gate = silu(gate_ref[:, pl.ds(where, cols)].astype(f32))
    if len(refs) == 2:
        out_ref, next_ref = refs
        out_ref[...] = total * gate
        next_ref[...] = factors[2 * tok :] * gate
        return
    _, own_sum_ref, own_factor_ref, own_top_ref, out_ref, own_ref = refs
    out_ref[...] = total * gate
    read = dot(queries, own_top_ref[...], ((1,), (0,)))
    own_ref[...] = own_sum_ref[...] + read * own_factor_ref[...]


def final_kernel(
    dims, lengths, group, queries_ref, own_ref, done_ref, one_sum, one_factor, one_top, two_sum,
    two_factor, two_top, gain_ref, out_hbm, gated_ref, out_ref, sems,
):
    count, masks, chunks = dims
    place = lax.rem(group[0], PLACES)
    tok, cols = own_ref.shape
    queries = queries_ref[...]
    squares = jnp.zeros((tok, LANES), f32)
    for at, (total, factor, top) in enumerate(
        (
            (own_ref, None, None),
            (done_ref, None, None),
            (one_sum, one_factor, one_top),
            (two_sum, two_factor, two_top),
        )
    ):
        value = total[...]
        if top is not None:
            value = value + dot(queries, top[...], ((1,), (0,))) * factor[...]
            gated_ref[at - 2] = value
        for lo in range(0, cols, LANES):
            squares = squares + value[:, lo : lo + LANES] * value[:, lo : lo + LANES]
    mean = jnp.sum(squares, axis=1, keepdims=True) / count
    scale = lax.rsqrt(mean + eps_norm)
    rows = tok // chunks
    copies = []
    for chunk in range(chunks):
        here = slice(chunk * rows, (chunk + 1) * rows)
        for at, mask in enumerate(masks):
            where = pl.multiple_of(jnp.bitwise_xor(place, mask) * cols, LANES)
            value = (own_ref[here], done_ref[here])[at] if at < 2 else gated_ref[at - 2, here]
            out_ref[here, pl.ds(where, cols)] = (
                value * scale[here] * gain_ref[:, pl.ds(where, cols)]
            ).astype(bf16)
        copy = pltpu.make_async_copy(out_ref.at[here], out_hbm.at[here], sems.at[chunk])
        copy.start()
        copies.append(copy)
    for copy in copies:
        copy.wait()


VMEM = pl.BlockSpec(memory_space=pltpu.VMEM)
HBM = pl.BlockSpec(memory_space=pltpu.HBM)
SMEM = pl.BlockSpec(memory_space=pltpu.SMEM)


def call(
    kernel, scalars, operands, outs, scratch=(), flops=0, specs=None, out_specs=None, grid=(), mb=40, after=()
):
    moved = sum(a.size * a.dtype.itemsize for a in operands)
    moved += sum(o.size * o.dtype.itemsize for o in outs)
    specs = list(specs or [VMEM] * len(operands))
    first, last = len(scalars) + len(operands), len(scalars) + len(operands) + len(after)

    def body(*refs):
        kernel(*refs[:first], *refs[last:])

    return pl.pallas_call(
        body,
        grid=grid,
        in_specs=[SMEM] * len(scalars) + specs + [pl.BlockSpec(memory_space=pl.ANY)] * len(after),
        out_specs=out_specs or [VMEM] * len(outs),
        scratch_shapes=list(scratch),
        out_shape=outs,
        compiler_params=pltpu.CompilerParams(vmem_limit_bytes=mb * 2**20),
        cost_estimate=pl.CostEstimate(
            flops=flops, bytes_accessed=moved, transcendentals=0
        ),
    )(*scalars, *operands, *after)


def shape(dims, dtype):
    return jax.ShapeDtypeStruct(dims, dtype)


def per_device(
    mixed_input,
    conv_weight,
    conv_bias,
    gate_input,
    log_decay,
    level_weights,
    skip_gain,
    norm_gain,
    seg_lengths,
):
    tok, channels = mixed_input.shape
    width = gate_input.shape[1]
    heads = log_decay.shape[0]
    head_dim = width // heads
    state = (channels - width) // 2
    taps = conv_weight.shape[0]
    recordings = seg_lengths.shape[0]
    low_bits = tok.bit_length() - 1
    groups = lax.axis_size("group")
    high_bits = groups.bit_length() - 1
    group = lax.axis_index("group").astype(jnp.int32)
    place = group % PLACES
    cols = width // PLACES
    block = 2 * state
    levels = jnp.transpose(level_weights, (1, 0, 2))

    def send(value, pairs):
        return lax.ppermute(value, "group", pairs)

    def quad_send(value, mask, wanted=lambda source, target: True):
        pairs = [(g, g ^ mask) for g in range(groups) if wanted(g, g ^ mask)]
        return send(value, pairs)

    halo = send(mixed_input[tok - HALO :], [(g, g + 1) for g in range(groups - 1)])

    def in_hbm(value):
        return pltpu.with_memory_space_constraint(value, pltpu.HBM)

    xs, kq, part, cum, cumt, entry, head, weights, first, lengths = call(
        functools.partial(
            features_kernel, (tok, heads, head_dim, taps, recordings, width, state)
        ),
        (group[None],),
        (
            in_hbm(mixed_input),
            in_hbm(conv_weight),
            in_hbm(conv_bias),
            in_hbm(log_decay),
            in_hbm(seg_lengths),
        ),
        [
            shape((tok, width), bf16),
            shape((tok, block), bf16),
            shape((state, width), f32),
            shape((heads, tok), f32),
            shape((tok, LANES), f32),
            shape((heads, tok), f32),
            shape((HALO, channels), bf16),
            shape((8, channels), f32),
            shape((HALO, width), f32),
            shape((recordings,), jnp.int32),
        ],
        [
            pltpu.VMEM((tok, channels), bf16),
            pltpu.VMEM((heads, tok), f32),
            pltpu.VMEM(((taps - 1) * tok, tok), bf16),
            pltpu.VMEM((tok, width), bf16),
            pltpu.SemaphoreType.DMA((5,)),
        ],
        flops=2 * tok * width * state,
        specs=[HBM] * 5,
        out_specs=[VMEM] * 9 + [SMEM],
    )
    scalars = (lengths, group[None])

    payload = shape((state + HALO, cols), bf16)
    px, pkq, own, one, two, three = call(
        functools.partial(join_kernel, (tok, taps, recordings, width, state)),
        scalars,
        (halo, head, weights, first, cumt, part),
        [shape((HALO, width), bf16), shape((HALO, block), bf16)] + [payload] * PLACES,
        [pltpu.VMEM((HALO, width), bf16)],
        flops=2 * HALO * width * state,
    )

    queries, scores, parts, coefs = call(
        functools.partial(shared_kernel, (tok, recordings, state, low_bits + 1)),
        scalars,
        (kq, pkq, cumt, levels, entry),
        [
            shape((tok, state), bf16),
            shape((tok, tok), f32),
            shape((tok, 3 * LANES), bf16),
            shape((3, tok, LANES), f32),
        ],
        flops=2 * tok * tok * state,
    )

    def local(mask, after=()):
        return call(
            functools.partial(local_kernel, (tok, head_dim, low_bits), mask),
            scalars,
            (xs, px, scores, cum, parts, levels, skip_gain),
            [shape((tok, cols), f32)],
            [pltpu.VMEM((2, tok, tok), bf16), pltpu.VMEM((tok, cols // head_dim * LANES), f32)],
            specs=[VMEM] * 6 + [SMEM],
            flops=2 * cols * tok * tok,
            after=after,
        )[0]

    got_three = quad_send(three, 3)
    got_one = quad_send(one, 1)
    got_two = quad_send(two, 2)
    sums = [local(0), local(1)]
    received = (own, got_one, got_two, got_three)
    quad, scale, spread_weights = call(
        functools.partial(combine_kernel, (state, head_dim)),
        scalars,
        received,
        [shape((state, cols), bf16), shape((8, LANES), f32), shape((8, cols), f32)],
        flops=4 * state * cols,
        after=sums,
    )
    pair, beside, across = call(
        functools.partial(pair_kernel, (state,)),
        scalars,
        received + (spread_weights, two),
        [
            shape((state, cols), bf16),
            shape((3 * state, cols), bf16),
            shape((2 * state, cols), bf16),
        ],
        flops=4 * state * cols,
        after=(quad,),
    )
    sums.append(local(2, (quad,)))
    sums.append(local(3, ()))
    got_three_of_pair = quad_send(pair, 3, lambda source, target: target & 2)
    got_beside = quad_send(beside, 1)
    got_across = quad_send(across, 2)

    lows = [(got_one, 0), (got_beside, 0), (got_across, state), (got_beside, state)]
    pairs = [(pair, 0), (got_beside, 2 * state), (got_across, 0), (got_three_of_pair, 0)]

    def far_part(mask, more=(), after=()):
        return list(
            call(
                functools.partial(far_kernel, (head_dim, state, lows[mask][1], pairs[mask][1]), mask),
                scalars,
                (sums[mask], queries, coefs, scale, lows[mask][0], pairs[mask][0], gate_input) + more,
                [shape((tok, cols), f32), shape((tok, cols), f32)],
                flops=int(2 * 1.1e9),
                after=after,
            )
        )

    halves = {0: far_part(0)}

    befores = [scale[0, :heads], scale[1, :heads], scale[2, :heads]]
    crossed = []
    running, total = quad, scale[3, :heads]
    for bit in range(2, high_bits):
        mask = 2**bit
        last = bit + 1 == high_bits
        far = quad_send(running, mask, lambda source, target: True)
        crossed.append(lax.optimization_barrier((far, sums[3], sums[2], halves[0][0]))[0])
        if not last:
            on_top = group // mask % 2 == 1
            far_total = quad_send(total, mask)

            def columns(value):
                mine = lax.dynamic_slice(value, (place * (cols // head_dim),), (cols // head_dim,))
                return jnp.repeat(mine, head_dim)[None, :]

            running = jnp.where(
                on_top,
                far.astype(f32) * columns(total) + running.astype(f32),
                running.astype(f32) * columns(far_total) + far.astype(f32),
            ).astype(bf16)
            befores.append(jnp.where(on_top, far_total * befores[-1], befores[-1]))
            total = total * far_total

    def all_quarters(value, bit):
        return [value] + [
            quad_send(value, mask)
            for mask in range(1, PLACES)
        ]

    tops = [all_quarters(value, bit + 2) for bit, value in enumerate(crossed)]
    halves[2] = far_part(2)
    halves[1] = far_part(1, after=halves[2][:1])
    extra = {mask: [] for mask in range(PLACES)}
    for bit in range(3, high_bits):
        coef = levels[low_bits + 1 + bit] * entry
        coef = coef * jnp.where(group // 2**bit % 2 == 1, befores[bit], 0.0)[:, None]
        for mask in range(PLACES):
            first_head = (place ^ mask) * (cols // head_dim)
            mine = lax.dynamic_slice_in_dim(coef, first_head, cols // head_dim, axis=0)
            gate = lax.dynamic_slice_in_dim(gate_input, (place ^ mask) * cols, cols, axis=1)
            read = jnp.dot(queries, tops[bit - 2][mask], preferred_element_type=f32)
            read = read * jnp.repeat(mine, head_dim, axis=0).T
            extra[mask].append(read * jax.nn.silu(gate.astype(f32)))
    for mask in halves:
        halves[mask][0] = sum(extra[mask], halves[mask][0])
    done, own_done = far_part(3, (tops[0][3], halves[0][0], halves[0][1], tops[0][0]), halves[1][:1])
    done = sum(extra[3], done)

    chunks = 4
    return call(
        functools.partial(final_kernel, (float(width), (0, 3, 1, 2), chunks)),
        scalars,
        (
            queries,
            own_done,
            done,
            halves[1][0],
            halves[1][1],
            tops[0][1],
            halves[2][0],
            halves[2][1],
            tops[0][2],
            norm_gain[None, :],
        ),
        [shape((tok, width), bf16)],
        [
            pltpu.VMEM((2, tok, cols), f32),
            pltpu.VMEM((tok, width), bf16),
            pltpu.SemaphoreType.DMA((chunks,)),
        ],
        out_specs=[HBM],
        flops=2 * tok * width * state,
    )[0]


def solution(mesh):
    in_specs = (
        P(("batch", "group"), None),
        P(),
        P(),
        P(("batch", "group"), None),
        P(None, ("batch", "group")),
        P(None, None, ("batch", "group")),
        P(),
        P(),
        P("batch"),
    )
    out_specs = P(("batch", "group"), None)
    return jax.shard_map(
        per_device, mesh=mesh, in_specs=in_specs, out_specs=out_specs, check_vma=False
    )
```

```python
import functools

import jax
import jax.numpy as jnp
from jax import lax
from jax.experimental import pallas as pl
from jax.experimental.pallas import tpu as pltpu
from jax.sharding import PartitionSpec as P

eps_norm = 1e-05
bf16 = jnp.bfloat16
f32 = jnp.float32
HALO = 16
PLACES = 4
LANES = 128


def iota(shape, dim):
    return lax.broadcasted_iota(jnp.int32, shape, dim)


def dot(a, b, contract, precision=None):
    return lax.dot_general(
        a, b, (contract, ((), ())), precision=precision, preferred_element_type=f32
    )


def silu(v):
    return v * (0.5 * jnp.tanh(0.5 * v) + 0.5)


def segment_bounds(lengths, recordings):
    bounds, total = [], 0
    for index in range(recordings - 1):
        total = total + lengths[index]
        bounds.append(total)
    return bounds


def segment_of(pos, bounds):
    found = jnp.where(pos >= 0, 0, -1)
    for bound in bounds:
        found = found + jnp.where(pos >= bound, 1, 0)
    return found


def same_segment(pos, other, bounds):
    return (segment_of(pos, bounds) == segment_of(other, bounds)).astype(f32)


def two_parts(value):
    high = value.astype(bf16).astype(f32)
    return high, value - high


def spread(rows, first_head, columns, head_dim):
    offset = iota((rows, LANES), 0) - iota((rows, LANES), 1) // head_dim
    tiles = []
    for tile in range(columns // LANES):
        tiles.append(
            jnp.where(offset == first_head + tile * (LANES // head_dim), 1.0, 0.0).astype(bf16)
        )
    return jnp.concatenate(tiles, axis=1)


def conv_taps(shifts, weight_ref, lo, hi):
    taps = len(shifts)
    total = weight_ref[taps : taps + 1, lo:hi]
    for tap, piece in enumerate(shifts):
        total = total + weight_ref[tap : tap + 1, lo:hi] * piece
    return silu(total)


def features_kernel(
    dims, group, x_hbm, w_hbm, b_hbm, decay_hbm, lengths_hbm,
    xs_ref, kq_ref, part_ref, cum_ref, cumt_ref, entry_ref, head_ref, weight_ref, first_ref,
    lengths, x_ref, decay_ref, shift_ref, scaled_ref, sems,
):
    tok, heads, head_dim, taps, recordings, width, state = dims
    block = 2 * state
    fetches = [
        pltpu.make_async_copy(source, target, sems.at[at])
        for at, (source, target) in enumerate(
            (
                (lengths_hbm, lengths),
                (decay_hbm, decay_ref),
                (x_hbm, x_ref),
                (w_hbm, weight_ref.at[:taps]),
                (b_hbm, weight_ref.at[taps]),
            )
        )
    ]
    for fetch in fetches:
        fetch.start()

    apart = iota((tok, tok), 0) - iota((tok, tok), 1)
    upper = jnp.where(apart <= 0, 1.0, 0.0).astype(bf16)
    lower = jnp.where(apart >= 0, 1.0, 0.0).astype(bf16)
    fetches[0].wait()
    bounds = segment_bounds(lengths, recordings)
    first = group[0] * tok
    pos = first + iota((tok, LANES), 0)
    for tap in range(1, taps):
        same = same_segment(pos, pos - tap, bounds)
        same = jnp.concatenate([same] * (tok // LANES), axis=1)
        shift_ref[(tap - 1) * tok : tap * tok] = jnp.where(apart == tap, same, 0.0).astype(bf16)
    fetches[1].wait()
    pad = jnp.zeros((LANES - heads, tok), f32)
    high, rest = two_parts(jnp.concatenate([decay_ref[...], pad], axis=0))
    mid, low = two_parts(rest)
    parts = jnp.concatenate([high, mid, low], axis=0).astype(bf16)
    cum = dot(parts, upper, ((1,), (0,)))
    cum = cum[:heads] + cum[LANES : LANES + heads] + cum[2 * LANES : 2 * LANES + heads]
    cum_ref[...] = cum
    cumt = dot(lower, parts, ((1,), (1,)))
    cumt = cumt[:, :LANES] + cumt[:, LANES : 2 * LANES] + cumt[:, 2 * LANES :]
    cumt_ref[...] = cumt
    end = cumt[tok - 1 : tok, :]
    last = first + tok - 1
    ewt = jnp.exp(end - cumt) * same_segment(pos, last + 0 * pos, bounds)
    along = first + iota((heads, tok), 1)
    entry_ref[...] = jnp.exp(cum) * same_segment(along, first - 1 + 0 * along, bounds)
    ewt = jnp.concatenate(two_parts(ewt), axis=1).astype(bf16)
    for fetch in fetches[2:]:
        fetch.wait()

    head_ref[...] = x_ref[:HALO]
    keys = None
    for at in [width // block] + list(range(width // block)):
        lo = at * block
        rows = x_ref[:, lo : lo + block]
        moved = dot(shift_ref[...], rows, ((1,), (0,)))
        shifts = [rows.astype(f32)]
        for tap in range(1, taps):
            shifts.append(moved[(tap - 1) * tok : tap * tok])
        value = conv_taps(shifts, weight_ref, lo, lo + block)
        if keys is None:
            kq_ref[...] = value.astype(bf16)
            keys = jnp.transpose(value[:, :state])
            keys = jnp.where(iota((state, tok), 1) >= HALO, keys, 0.0).astype(bf16)
            continue
        xs = value.astype(bf16)
        xs_ref[:, lo : lo + block] = xs
        copies = spread(LANES, lo // head_dim, block, head_dim)
        weight = dot(ewt, jnp.concatenate([copies, copies], axis=0), ((1,), (0,)))
        first_ref[:, lo : lo + block] = weight[:HALO]
        scaled_ref[:, lo : lo + block] = (xs.astype(f32) * weight).astype(bf16)
    part_ref[...] = dot(keys, scaled_ref[...], ((1,), (0,)))


def join_kernel(
    dims, lengths, group, halo_ref, head_ref, w_ref, first_ref, cumt_ref, part_ref,
    px_ref, pkq_ref, own_ref, one_ref, two_ref, three_ref, scaled_ref,
):
    tok, taps, recordings, width, state = dims
    bounds = segment_bounds(lengths, recordings)
    first = group[0] * tok
    pos = first + iota((HALO, LANES), 0)
    same = [same_segment(pos, pos - tap, bounds) for tap in range(1, taps)]

    def features(lo):
        hi = lo + LANES
        both = jnp.concatenate(
            [halo_ref[:, lo:hi].astype(f32), head_ref[:, lo:hi].astype(f32)], axis=0
        )
        shifts = [both[HALO:]] + [
            pltpu.roll(both, tap, 0)[HALO:] * same[tap - 1] for tap in range(1, taps)
        ]
        return conv_taps(shifts, w_ref, lo, hi)

    keys = None
    for lo in range(width, width + 2 * state, LANES):
        part = features(lo).astype(bf16)
        pkq_ref[:, lo - width : lo - width + LANES] = part
        if lo == width:
            keys = part
    for lo in range(0, width, LANES):
        xs = features(lo).astype(bf16)
        px_ref[:, lo : lo + LANES] = xs
        scaled_ref[:, lo : lo + LANES] = (
            xs.astype(f32) * first_ref[:, lo : lo + LANES]
        ).astype(bf16)

    end = cumt_ref[tok - 1 : tok, :]
    alive = same_segment(first + tok - 1 + 0 * pos[:1], first - 1 + 0 * pos[:1], bounds)
    through = jnp.exp(end) * alive
    high, rest = two_parts(through)
    mid, low = two_parts(rest)
    row = iota((HALO, LANES), 0)
    tail = jnp.where(row == 0, high, jnp.where(row == 1, mid, jnp.where(row == 2, low, 0.0)))
    place = lax.rem(group[0], PLACES)
    cols = width // PLACES
    for mask, out_ref in ((3, three_ref), (1, one_ref), (2, two_ref), (0, own_ref)):
        where = pl.multiple_of(jnp.bitwise_xor(place, mask) * cols, LANES)
        value = part_ref[:, pl.ds(where, cols)] + dot(
            keys, scaled_ref[:, pl.ds(where, cols)], ((0,), (0,))
        )
        out_ref[:state, :] = value.astype(bf16)
        out_ref[state:, :LANES] = tail.astype(bf16)
        out_ref[state:, LANES:] = jnp.zeros((HALO, cols - LANES), bf16)


def combine_kernel(
    dims, lengths, group, own_ref, one_ref, two_ref, three_ref, quad_ref, scale_ref, weight_ref
):
    state, head_dim = dims
    cols = quad_ref.shape[1]
    place = lax.rem(group[0], PLACES)
    refs = (own_ref, one_ref, two_ref, three_ref)
    got = []
    for ref in refs:
        tail = ref[state:, :LANES].astype(f32)
        got.append(tail[0:1] + tail[1:2] + tail[2:3])
    through = []
    for at in range(PLACES):
        total = jnp.zeros((1, LANES), f32)
        for mask in range(PLACES):
            total = total + jnp.where(jnp.bitwise_xor(place, mask) == at, got[mask], 0.0)
        through.append(total)
    ones = jnp.ones((1, LANES), f32)
    rows = []
    for mask in range(PLACES):
        at = jnp.bitwise_xor(place, mask)
        product = ones
        for later in range(1, PLACES):
            product = product * jnp.where(later > at, through[later], ones)
        rows.append(product)
    for mask in range(PLACES):
        at = jnp.bitwise_xor(place, mask)
        rows.append(jnp.where(at == 0, through[1], jnp.where(at == 1, ones, 0.0 * ones)))
    before_quad = ones
    for earlier in range(PLACES - 1):
        before_quad = before_quad * jnp.where(earlier < place, through[earlier], ones)
    everything = through[0] * through[1] * through[2] * through[3]
    row = iota((8, LANES), 0)
    scale = jnp.where(row == 1, jnp.where(place == 3, through[2], ones), ones)
    scale = jnp.where(row == 2, before_quad, scale)
    scale_ref[...] = jnp.where(row == 3, everything, scale)
    weights = jnp.concatenate(rows, axis=0)
    high, low = two_parts(weights)
    copies = spread(LANES, place * (cols // head_dim), cols, head_dim)
    weights = dot(high.astype(bf16), copies, ((1,), (0,))) + dot(
        low.astype(bf16), copies, ((1,), (0,))
    )
    weight_ref[...] = weights
    for lo in range(0, cols, LANES):
        hi = lo + LANES
        quad = jnp.zeros((state, LANES), f32)
        for mask, ref in enumerate(refs):
            quad = quad + ref[:state, lo:hi].astype(f32) * weights[mask : mask + 1, lo:hi]
        quad_ref[:, lo:hi] = quad.astype(bf16)


def pair_kernel(
    dims, lengths, group, own_ref, one_ref, two_ref, three_ref, weight_ref, two_in,
    pair_ref, beside_ref, across_ref,
):
    (state,) = dims
    cols = pair_ref.shape[1]
    beside_ref[:state] = own_ref[:state]
    beside_ref[state : 2 * state] = two_in[:state]
    across_ref[state:] = three_ref[:state]
    for lo in range(0, cols, LANES):
        hi = lo + LANES
        pair = jnp.zeros((state, LANES), f32)
        for mask, ref in enumerate((own_ref, one_ref, two_ref, three_ref)):
            weight = weight_ref[PLACES + mask : PLACES + mask + 1, lo:hi]
            pair = pair + ref[:state, lo:hi].astype(f32) * weight
        pair = pair.astype(bf16)
        pair_ref[:, lo:hi] = pair
        across_ref[:state, lo:hi] = pair
        beside_ref[2 * state :, lo:hi] = pair


def with_head(patch, body):
    return jnp.concatenate([patch, body[HALO:]], axis=0)


def shared_kernel(
    dims, lengths, group, kq_ref, pkq_ref, cumt_ref, level_ref, entry_ref,
    queries_ref, scores_ref, parts_ref, coef_ref,
):
    tok, recordings, state, far_from = dims
    heads = entry_ref.shape[0]
    bounds = segment_bounds(lengths, recordings)
    first = group[0] * tok
    kq = with_head(pkq_ref[...], kq_ref[...])
    queries_ref[...] = kq[:, state:]
    s_pos = iota((tok, tok), 0)
    t_pos = iota((tok, tok), 1)
    valid = same_segment(first + s_pos, first + t_pos, bounds) * jnp.where(s_pos <= t_pos, 1.0, 0.0)
    scores_ref[...] = dot(kq[:, :state], kq[:, state:], ((1,), (1,))) * valid
    high, rest = two_parts(cumt_ref[...])
    mid, low = two_parts(rest)
    parts_ref[...] = jnp.concatenate([high, mid, low], axis=1).astype(bf16)
    for bit in range(coef_ref.shape[0]):
        coef = level_ref[far_from + bit] * entry_ref[...]
        coef = jnp.concatenate([coef, jnp.zeros((LANES - heads, tok), f32)], axis=0)
        coef_ref[bit] = jnp.transpose(coef)


def local_kernel(
    dims, mask, lengths, group, xs_ref, px_ref, scores_ref, cum_ref, parts_ref, level_ref, skip_ref,
    out_ref, mixing_ref, copied_ref,
):
    tok, head_dim, low_bits = dims
    cols = out_ref.shape[1]
    count = cols // head_dim
    quarter = jnp.bitwise_xor(lax.rem(group[0], PLACES), mask)
    first_head = quarter * count
    rows = 32
    row_bits = rows.bit_length() - 1
    where = pl.multiple_of(quarter * cols, LANES)
    copies = spread(LANES, first_head, count * LANES, LANES)
    copied_ref[...] = dot(parts_ref[...], jnp.concatenate([copies] * 3, axis=0), ((1,), (0,)))
    diff = jnp.bitwise_xor(iota((rows, tok), 0), lax.rem(iota((rows, tok), 1), rows))
    near = jnp.zeros((rows, tok), jnp.int32)
    for bit in range(row_bits):
        near = near + (diff >= 2**bit).astype(jnp.int32)
    token = iota((1, tok), 1) // rows
    lane = iota((1, 2 * head_dim), 1)
    unit = jnp.where(iota((tok, tok), 0) == iota((tok, tok), 1), 1.0, 0.0).astype(bf16)
    mixing_ref[...] = jnp.zeros(mixing_ref.shape, bf16)
    pieces = []
    for head in range(count):
        if head % 2 == 0:
            lo = head * head_dim
            here = pl.ds(pl.multiple_of(where + lo, LANES), 2 * head_dim)
            xs = with_head(px_ref[:, here], xs_ref[:, here])
            xst = jnp.transpose(xs)
        cum = cum_ref[pl.ds(first_head + head, 1), :]
        levels = [level_ref[level, pl.ds(first_head + head, 1), :] for level in range(low_bits + 1)]
        inner = jnp.broadcast_to(levels[0], (rows, tok))
        for level in range(1, row_bits + 1):
            inner = jnp.where(near == level, levels[level], inner)
        for s in range(0, tok, rows):
            at = s // rows
            outer = jnp.zeros((1, tok), f32)
            apart = jnp.bitwise_xor(token, at)
            for level in range(row_bits + 1, low_bits + 1):
                outer = jnp.where(apart >= 2 ** (level - row_bits - 1), levels[level], outer)
            before = copied_ref[s : s + rows, head * LANES : (head + 1) * LANES]
            for t in range(s // LANES * LANES, tok, LANES):
                here_t = slice(t, t + LANES)
                picked = outer[:, here_t]
                gap = cum[:, here_t] - before
                if t <= s:
                    picked = jnp.where(token[:, here_t] == at, inner[:, here_t], picked)
                    gap = jnp.minimum(gap, 0.0)
                mixing_ref[head % 2, s : s + rows, here_t] = (
                    jnp.exp(gap) * picked * scores_ref[s : s + rows, here_t]
                ).astype(bf16)
        pieces.append(
            dot(
                xst[head % 2 * head_dim : (head % 2 + 1) * head_dim],
                mixing_ref[head % 2],
                ((1,), (0,)),
            )
        )
        if head % 2 == 1:
            both = jnp.concatenate(pieces[-2:], axis=0)
            skip = jnp.where(
                lane < head_dim, skip_ref[first_head + head - 1], skip_ref[first_head + head]
            )
            out_ref[:, lo : lo + 2 * head_dim] = jnp.transpose(both) + skip * xs.astype(f32)


def far_kernel(
    dims, mask, lengths, group, sum_ref, queries_ref, coef_ref, scale_ref, low_ref,
    pair_ref, gate_ref, *refs,
):
    head_dim, state, low_from, pair_from = dims
    tok, cols = sum_ref.shape
    quarter = jnp.bitwise_xor(lax.rem(group[0], PLACES), mask)
    first = quarter * (cols // head_dim)
    queries = queries_ref[...]
    coefs = []
    for bit in range(coef_ref.shape[0]):
        on = jnp.where(lax.rem(group[0] // 2**bit, 2) == 1, 1.0, 0.0)
        coef = two_parts(coef_ref[bit] * (scale_ref[bit : bit + 1, :] * on))
        coefs.append(jnp.concatenate(coef, axis=1).astype(bf16))
    copies = spread(LANES, first, cols, head_dim)
    factors = dot(
        jnp.concatenate(coefs, axis=0), jnp.concatenate([copies, copies], axis=0), ((1,), (0,))
    )
    total = sum_ref[...]
    states = [low_ref[low_from : low_from + state], pair_ref[pair_from : pair_from + state]]
    if len(refs) > 2:
        states.append(refs[0][...])
    for bit, state_in in enumerate(states):
        total = total + dot(queries, state_in, ((1,), (0,))) * factors[bit * tok : (bit + 1) * tok]
    where = pl.multiple_of(quarter * cols, LANES)
    gate = silu(gate_ref[:, pl.ds(where, cols)].astype(f32))
    if len(refs) == 2:
        out_ref, next_ref = refs
        out_ref[...] = total * gate
        next_ref[...] = factors[2 * tok :] * gate
        return
    _, own_sum_ref, own_factor_ref, own_top_ref, out_ref, own_ref = refs
    out_ref[...] = total * gate
    read = dot(queries, own_top_ref[...], ((1,), (0,)))
    own_ref[...] = own_sum_ref[...] + read * own_factor_ref[...]


def final_kernel(
    dims, lengths, group, queries_ref, own_ref, done_ref, one_sum, one_factor, one_top, two_sum,
    two_factor, two_top, gain_ref, out_hbm, gated_ref, out_ref, sems,
):
    count, masks, chunks = dims
    place = lax.rem(group[0], PLACES)
    tok, cols = own_ref.shape
    queries = queries_ref[...]
    squares = jnp.zeros((tok, LANES), f32)
    for at, (total, factor, top) in enumerate(
        (
            (own_ref, None, None),
            (done_ref, None, None),
            (one_sum, one_factor, one_top),
            (two_sum, two_factor, two_top),
        )
    ):
        value = total[...]
        if top is not None:
            value = value + dot(queries, top[...], ((1,), (0,))) * factor[...]
            gated_ref[at - 2] = value
        for lo in range(0, cols, LANES):
            squares = squares + value[:, lo : lo + LANES] * value[:, lo : lo + LANES]
    mean = jnp.sum(squares, axis=1, keepdims=True) / count
    scale = lax.rsqrt(mean + eps_norm)
    rows = tok // chunks
    copies = []
    for chunk in range(chunks):
        here = slice(chunk * rows, (chunk + 1) * rows)
        for at, mask in enumerate(masks):
            where = pl.multiple_of(jnp.bitwise_xor(place, mask) * cols, LANES)
            value = (own_ref[here], done_ref[here])[at] if at < 2 else gated_ref[at - 2, here]
            out_ref[here, pl.ds(where, cols)] = (
                value * scale[here] * gain_ref[:, pl.ds(where, cols)]
            ).astype(bf16)
        copy = pltpu.make_async_copy(out_ref.at[here], out_hbm.at[here], sems.at[chunk])
        copy.start()
        copies.append(copy)
    for copy in copies:
        copy.wait()


VMEM = pl.BlockSpec(memory_space=pltpu.VMEM)
HBM = pl.BlockSpec(memory_space=pltpu.HBM)
SMEM = pl.BlockSpec(memory_space=pltpu.SMEM)


def call(
    kernel, scalars, operands, outs, scratch=(), flops=0, specs=None, out_specs=None, grid=(), mb=40, after=()
):
    moved = sum(a.size * a.dtype.itemsize for a in operands)
    moved += sum(o.size * o.dtype.itemsize for o in outs)
    specs = list(specs or [VMEM] * len(operands))
    first, last = len(scalars) + len(operands), len(scalars) + len(operands) + len(after)

    def body(*refs):
        kernel(*refs[:first], *refs[last:])

    return pl.pallas_call(
        body,
        grid=grid,
        in_specs=[SMEM] * len(scalars) + specs + [pl.BlockSpec(memory_space=pl.ANY)] * len(after),
        out_specs=out_specs or [VMEM] * len(outs),
        scratch_shapes=list(scratch),
        out_shape=outs,
        compiler_params=pltpu.CompilerParams(vmem_limit_bytes=mb * 2**20),
        cost_estimate=pl.CostEstimate(
            flops=flops, bytes_accessed=moved, transcendentals=0
        ),
    )(*scalars, *operands, *after)


def shape(dims, dtype):
    return jax.ShapeDtypeStruct(dims, dtype)


def per_device(
    mixed_input,
    conv_weight,
    conv_bias,
    gate_input,
    log_decay,
    level_weights,
    skip_gain,
    norm_gain,
    seg_lengths,
):
    tok, channels = mixed_input.shape
    width = gate_input.shape[1]
    heads = log_decay.shape[0]
    head_dim = width // heads
    state = (channels - width) // 2
    taps = conv_weight.shape[0]
    recordings = seg_lengths.shape[0]
    low_bits = tok.bit_length() - 1
    groups = lax.axis_size("group")
    high_bits = groups.bit_length() - 1
    group = lax.axis_index("group").astype(jnp.int32)
    place = group % PLACES
    cols = width // PLACES
    block = 2 * state
    levels = jnp.transpose(level_weights, (1, 0, 2))

    def send(value, pairs):
        return lax.ppermute(value, "group", pairs)

    def quad_send(value, mask, wanted=lambda source, target: True):
        pairs = [(g, g ^ mask) for g in range(groups) if wanted(g, g ^ mask)]
        return send(value, pairs)

    halo = send(mixed_input[tok - HALO :], [(g, (g + 1) % groups) for g in range(groups)])

    def in_hbm(value):
        return pltpu.with_memory_space_constraint(value, pltpu.HBM)

    xs, kq, part, cum, cumt, entry, head, weights, first, lengths = call(
        functools.partial(
            features_kernel, (tok, heads, head_dim, taps, recordings, width, state)
        ),
        (group[None],),
        (
            in_hbm(mixed_input),
            in_hbm(conv_weight),
            in_hbm(conv_bias),
            in_hbm(log_decay),
            in_hbm(seg_lengths),
        ),
        [
            shape((tok, width), bf16),
            shape((tok, block), bf16),
            shape((state, width), f32),
            shape((heads, tok), f32),
            shape((tok, LANES), f32),
            shape((heads, tok), f32),
            shape((HALO, channels), bf16),
            shape((8, channels), f32),
            shape((HALO, width), f32),
            shape((recordings,), jnp.int32),
        ],
        [
            pltpu.VMEM((tok, channels), bf16),
            pltpu.VMEM((heads, tok), f32),
            pltpu.VMEM(((taps - 1) * tok, tok), bf16),
            pltpu.VMEM((tok, width), bf16),
            pltpu.SemaphoreType.DMA((5,)),
        ],
        flops=2 * tok * width * state,
        specs=[HBM] * 5,
        out_specs=[VMEM] * 9 + [SMEM],
    )
    scalars = (lengths, group[None])

    payload = shape((state + HALO, cols), bf16)
    px, pkq, own, one, two, three = call(
        functools.partial(join_kernel, (tok, taps, recordings, width, state)),
        scalars,
        (halo, head, weights, first, cumt, part),
        [shape((HALO, width), bf16), shape((HALO, block), bf16)] + [payload] * PLACES,
        [pltpu.VMEM((HALO, width), bf16)],
        flops=2 * HALO * width * state,
    )

    queries, scores, parts, coefs = call(
        functools.partial(shared_kernel, (tok, recordings, state, low_bits + 1)),
        scalars,
        (kq, pkq, cumt, levels, entry),
        [
            shape((tok, state), bf16),
            shape((tok, tok), f32),
            shape((tok, 3 * LANES), bf16),
            shape((3, tok, LANES), f32),
        ],
        flops=2 * tok * tok * state,
    )

    def local(mask, after=()):
        return call(
            functools.partial(local_kernel, (tok, head_dim, low_bits), mask),
            scalars,
            (xs, px, scores, cum, parts, levels, skip_gain),
            [shape((tok, cols), f32)],
            [pltpu.VMEM((2, tok, tok), bf16), pltpu.VMEM((tok, cols // head_dim * LANES), f32)],
            specs=[VMEM] * 6 + [SMEM],
            flops=2 * cols * tok * tok,
            after=after,
        )[0]

    got_three = quad_send(three, 3)
    got_one = quad_send(one, 1)
    got_two = quad_send(two, 2)
    sums = [local(0), local(1)]
    received = (own, got_one, got_two, got_three)
    quad, scale, spread_weights = call(
        functools.partial(combine_kernel, (state, head_dim)),
        scalars,
        received,
        [shape((state, cols), bf16), shape((8, LANES), f32), shape((8, cols), f32)],
        flops=4 * state * cols,
        after=sums,
    )
    pair, beside, across = call(
        functools.partial(pair_kernel, (state,)),
        scalars,
        received + (spread_weights, two),
        [
            shape((state, cols), bf16),
            shape((3 * state, cols), bf16),
            shape((2 * state, cols), bf16),
        ],
        flops=4 * state * cols,
        after=(quad,),
    )
    sums.append(local(2, (quad,)))
    sums.append(local(3, ()))
    got_three_of_pair = quad_send(pair, 3, lambda source, target: target & 2)
    got_beside = quad_send(beside, 1)
    got_across = quad_send(across, 2)

    lows = [(got_one, 0), (got_beside, 0), (got_across, state), (got_beside, state)]
    pairs = [(pair, 0), (got_beside, 2 * state), (got_across, 0), (got_three_of_pair, 0)]

    def far_part(mask, more=(), after=()):
        return list(
            call(
                functools.partial(far_kernel, (head_dim, state, lows[mask][1], pairs[mask][1]), mask),
                scalars,
                (sums[mask], queries, coefs, scale, lows[mask][0], pairs[mask][0], gate_input) + more,
                [shape((tok, cols), f32), shape((tok, cols), f32)],
                flops=int(2 * 1.1e9),
                after=after,
            )
        )

    halves = {0: far_part(0)}

    befores = [scale[0, :heads], scale[1, :heads], scale[2, :heads]]
    crossed = []
    running, total = quad, scale[3, :heads]
    for bit in range(2, high_bits):
        mask = 2**bit
        last = bit + 1 == high_bits
        far = quad_send(running, mask, lambda source, target: True)
        crossed.append(lax.optimization_barrier((far, sums[3], sums[2], halves[0][0]))[0])
        if not last:
            on_top = group // mask % 2 == 1
            far_total = quad_send(total, mask)

            def columns(value):
                mine = lax.dynamic_slice(value, (place * (cols // head_dim),), (cols // head_dim,))
                return jnp.repeat(mine, head_dim)[None, :]

            running = jnp.where(
                on_top,
                far.astype(f32) * columns(total) + running.astype(f32),
                running.astype(f32) * columns(far_total) + far.astype(f32),
            ).astype(bf16)
            befores.append(jnp.where(on_top, far_total * befores[-1], befores[-1]))
            total = total * far_total

    def all_quarters(value, bit):
        return [value] + [
            quad_send(value, mask)
            for mask in range(1, PLACES)
        ]

    tops = [all_quarters(value, bit + 2) for bit, value in enumerate(crossed)]
    halves[2] = far_part(2)
    halves[1] = far_part(1, after=halves[2][:1])
    extra = {mask: [] for mask in range(PLACES)}
    for bit in range(3, high_bits):
        coef = levels[low_bits + 1 + bit] * entry
        coef = coef * jnp.where(group // 2**bit % 2 == 1, befores[bit], 0.0)[:, None]
        for mask in range(PLACES):
            first_head = (place ^ mask) * (cols // head_dim)
            mine = lax.dynamic_slice_in_dim(coef, first_head, cols // head_dim, axis=0)
            gate = lax.dynamic_slice_in_dim(gate_input, (place ^ mask) * cols, cols, axis=1)
            read = jnp.dot(queries, tops[bit - 2][mask], preferred_element_type=f32)
            read = read * jnp.repeat(mine, head_dim, axis=0).T
            extra[mask].append(read * jax.nn.silu(gate.astype(f32)))
    for mask in halves:
        halves[mask][0] = sum(extra[mask], halves[mask][0])
    done, own_done = far_part(3, (tops[0][3], halves[0][0], halves[0][1], tops[0][0]), halves[1][:1])
    done = sum(extra[3], done)

    chunks = 4
    return call(
        functools.partial(final_kernel, (float(width), (0, 3, 1, 2), chunks)),
        scalars,
        (
            queries,
            own_done,
            done,
            halves[1][0],
            halves[1][1],
            tops[0][1],
            halves[2][0],
            halves[2][1],
            tops[0][2],
            norm_gain[None, :],
        ),
        [shape((tok, width), bf16)],
        [
            pltpu.VMEM((2, tok, cols), f32),
            pltpu.VMEM((tok, width), bf16),
            pltpu.SemaphoreType.DMA((chunks,)),
        ],
        out_specs=[HBM],
        flops=2 * tok * width * state,
    )[0]


def solution(mesh):
    in_specs = (
        P(("batch", "group"), None),
        P(),
        P(),
        P(("batch", "group"), None),
        P(None, ("batch", "group")),
        P(None, None, ("batch", "group")),
        P(),
        P(),
        P("batch"),
    )
    out_specs = P(("batch", "group"), None)
    return jax.shard_map(
        per_device, mesh=mesh, in_specs=in_specs, out_specs=out_specs, check_vma=False
    )
```

```python
import functools

import jax
import jax.numpy as jnp
from jax import lax
from jax.experimental import pallas as pl
from jax.experimental.pallas import tpu as pltpu
from jax.sharding import PartitionSpec as P

eps_norm = 1e-05
bf16 = jnp.bfloat16
f32 = jnp.float32
HALO = 16
PLACES = 4
LANES = 128


def iota(shape, dim):
    return lax.broadcasted_iota(jnp.int32, shape, dim)


def dot(a, b, contract, precision=None):
    return lax.dot_general(
        a, b, (contract, ((), ())), precision=precision, preferred_element_type=f32
    )


def silu_of_half(h):
    return h * jnp.tanh(h) + h


def silu(v):
    return silu_of_half(0.5 * v)


def segment_bounds(lengths, recordings):
    bounds, total = [], 0
    for index in range(recordings - 1):
        total = total + lengths[index]
        bounds.append(total)
    return bounds


def segment_of(pos, bounds):
    found = jnp.where(pos >= 0, 0, -1)
    for bound in bounds:
        found = found + jnp.where(pos >= bound, 1, 0)
    return found


def same_segment(pos, other, bounds):
    return (segment_of(pos, bounds) == segment_of(other, bounds)).astype(f32)


def two_parts(value):
    high = value.astype(bf16).astype(f32)
    return high, value - high


def spread(rows, first_head, columns, head_dim):
    offset = iota((rows, LANES), 0) - iota((rows, LANES), 1) // head_dim
    tiles = []
    for tile in range(columns // LANES):
        tiles.append(
            jnp.where(offset == first_head + tile * (LANES // head_dim), 1.0, 0.0).astype(bf16)
        )
    return jnp.concatenate(tiles, axis=1)


def conv_taps(shifts, weight_ref, lo, hi):
    taps = len(shifts)
    total = weight_ref[taps : taps + 1, lo:hi]
    for tap, piece in enumerate(shifts):
        total = total + weight_ref[tap : tap + 1, lo:hi] * piece
    return silu_of_half(total)


def features_kernel(
    dims, group, x_hbm, w_hbm, b_hbm, decay_hbm, lengths_hbm,
    xs_ref, kq_ref, part_ref, cum_ref, cumt_ref, entry_ref, head_ref, weight_ref, first_ref,
    lengths, x_ref, decay_ref, shift_ref, scaled_ref, sems,
):
    tok, heads, head_dim, taps, recordings, width, state = dims
    block = 2 * state
    fetches = [
        pltpu.make_async_copy(source, target, sems.at[at])
        for at, (source, target) in enumerate(
            (
                (lengths_hbm, lengths),
                (decay_hbm, decay_ref),
                (x_hbm, x_ref),
                (w_hbm, weight_ref.at[:taps]),
                (b_hbm, weight_ref.at[taps]),
            )
        )
    ]
    for fetch in fetches:
        fetch.start()

    apart = iota((tok, tok), 0) - iota((tok, tok), 1)
    upper = jnp.where(apart <= 0, 1.0, 0.0).astype(bf16)
    lower = jnp.where(apart >= 0, 1.0, 0.0).astype(bf16)
    fetches[0].wait()
    bounds = segment_bounds(lengths, recordings)
    first = group[0] * tok
    pos = first + iota((tok, LANES), 0)
    for tap in range(1, taps):
        same = same_segment(pos, pos - tap, bounds)
        same = jnp.concatenate([same] * (tok // LANES), axis=1)
        shift_ref[(tap - 1) * tok : tap * tok] = jnp.where(apart == tap, same, 0.0).astype(bf16)
    fetches[1].wait()
    pad = jnp.zeros((LANES - heads, tok), f32)
    high, rest = two_parts(jnp.concatenate([decay_ref[...], pad], axis=0))
    mid, low = two_parts(rest)
    parts = jnp.concatenate([high, mid, low], axis=0).astype(bf16)
    cum = dot(parts, upper, ((1,), (0,)))
    cum = cum[:heads] + cum[LANES : LANES + heads] + cum[2 * LANES : 2 * LANES + heads]
    cum_ref[...] = cum
    cumt = dot(lower, parts, ((1,), (1,)))
    cumt = cumt[:, :LANES] + cumt[:, LANES : 2 * LANES] + cumt[:, 2 * LANES :]
    cumt_ref[...] = cumt
    end = cumt[tok - 1 : tok, :]
    last = first + tok - 1
    ewt = jnp.exp(end - cumt) * same_segment(pos, last + 0 * pos, bounds)
    along = first + iota((heads, tok), 1)
    entry_ref[...] = jnp.exp(cum) * same_segment(along, first - 1 + 0 * along, bounds)
    ewt = jnp.concatenate(two_parts(ewt), axis=1).astype(bf16)
    for fetch in fetches[2:]:
        fetch.wait()

    weight_ref[: taps + 1] = 0.5 * weight_ref[: taps + 1]
    head_ref[...] = x_ref[:HALO]
    keys = None
    for at in [width // block] + list(range(width // block)):
        lo = at * block
        rows = x_ref[:, lo : lo + block]
        moved = dot(shift_ref[...], rows, ((1,), (0,)))
        shifts = [rows.astype(f32)]
        for tap in range(1, taps):
            shifts.append(moved[(tap - 1) * tok : tap * tok])
        value = conv_taps(shifts, weight_ref, lo, lo + block)
        if keys is None:
            kq_ref[...] = value.astype(bf16)
            keys = jnp.transpose(value[:, :state])
            keys = jnp.where(iota((state, tok), 1) >= HALO, keys, 0.0).astype(bf16)
            continue
        xs = value.astype(bf16)
        xs_ref[:, lo : lo + block] = xs
        copies = spread(LANES, lo // head_dim, block, head_dim)
        weight = dot(ewt, jnp.concatenate([copies, copies], axis=0), ((1,), (0,)))
        first_ref[:, lo : lo + block] = weight[:HALO]
        scaled_ref[:, lo : lo + block] = (xs.astype(f32) * weight).astype(bf16)
    part_ref[...] = dot(keys, scaled_ref[...], ((1,), (0,)))


def join_kernel(
    dims, lengths, group, halo_ref, head_ref, w_ref, first_ref, cumt_ref, part_ref,
    px_ref, pkq_ref, own_ref, one_ref, two_ref, three_ref, scaled_ref,
):
    tok, taps, recordings, width, state = dims
    bounds = segment_bounds(lengths, recordings)
    first = group[0] * tok
    pos = first + iota((HALO, LANES), 0)
    same = [same_segment(pos, pos - tap, bounds) for tap in range(1, taps)]

    def features(lo):
        hi = lo + LANES
        both = jnp.concatenate(
            [halo_ref[:, lo:hi].astype(f32), head_ref[:, lo:hi].astype(f32)], axis=0
        )
        shifts = [both[HALO:]] + [
            pltpu.roll(both, tap, 0)[HALO:] * same[tap - 1] for tap in range(1, taps)
        ]
        return conv_taps(shifts, w_ref, lo, hi)

    keys = None
    for lo in range(width, width + 2 * state, LANES):
        part = features(lo).astype(bf16)
        pkq_ref[:, lo - width : lo - width + LANES] = part
        if lo == width:
            keys = part
    for lo in range(0, width, LANES):
        xs = features(lo).astype(bf16)
        px_ref[:, lo : lo + LANES] = xs
        scaled_ref[:, lo : lo + LANES] = (
            xs.astype(f32) * first_ref[:, lo : lo + LANES]
        ).astype(bf16)

    end = cumt_ref[tok - 1 : tok, :]
    alive = same_segment(first + tok - 1 + 0 * pos[:1], first - 1 + 0 * pos[:1], bounds)
    through = jnp.exp(end) * alive
    high, rest = two_parts(through)
    mid, low = two_parts(rest)
    row = iota((HALO, LANES), 0)
    tail = jnp.where(row == 0, high, jnp.where(row == 1, mid, jnp.where(row == 2, low, 0.0)))
    place = lax.rem(group[0], PLACES)
    cols = width // PLACES
    for mask, out_ref in ((3, three_ref), (1, one_ref), (2, two_ref), (0, own_ref)):
        where = pl.multiple_of(jnp.bitwise_xor(place, mask) * cols, LANES)
        value = part_ref[:, pl.ds(where, cols)] + dot(
            keys, scaled_ref[:, pl.ds(where, cols)], ((0,), (0,))
        )
        out_ref[:state, :] = value.astype(bf16)
        out_ref[state:, :LANES] = tail.astype(bf16)
        out_ref[state:, LANES:] = jnp.zeros((HALO, cols - LANES), bf16)


def combine_kernel(
    dims, lengths, group, own_ref, one_ref, two_ref, three_ref, quad_ref, scale_ref, weight_ref
):
    state, head_dim = dims
    cols = quad_ref.shape[1]
    place = lax.rem(group[0], PLACES)
    refs = (own_ref, one_ref, two_ref, three_ref)
    got = []
    for ref in refs:
        tail = ref[state:, :LANES].astype(f32)
        got.append(tail[0:1] + tail[1:2] + tail[2:3])
    through = []
    for at in range(PLACES):
        total = jnp.zeros((1, LANES), f32)
        for mask in range(PLACES):
            total = total + jnp.where(jnp.bitwise_xor(place, mask) == at, got[mask], 0.0)
        through.append(total)
    ones = jnp.ones((1, LANES), f32)
    rows = []
    for mask in range(PLACES):
        at = jnp.bitwise_xor(place, mask)
        product = ones
        for later in range(1, PLACES):
            product = product * jnp.where(later > at, through[later], ones)
        rows.append(product)
    for mask in range(PLACES):
        at = jnp.bitwise_xor(place, mask)
        rows.append(jnp.where(at == 0, through[1], jnp.where(at == 1, ones, 0.0 * ones)))
    before_quad = ones
    for earlier in range(PLACES - 1):
        before_quad = before_quad * jnp.where(earlier < place, through[earlier], ones)
    everything = through[0] * through[1] * through[2] * through[3]
    row = iota((8, LANES), 0)
    scale = jnp.where(row == 1, jnp.where(place == 3, through[2], ones), ones)
    scale = jnp.where(row == 2, before_quad, scale)
    scale_ref[...] = jnp.where(row == 3, everything, scale)
    weights = jnp.concatenate(rows, axis=0)
    high, low = two_parts(weights)
    copies = spread(LANES, place * (cols // head_dim), cols, head_dim)
    weights = dot(
        jnp.concatenate([high, low], axis=1).astype(bf16),
        jnp.concatenate([copies, copies], axis=0),
        ((1,), (0,)),
    )
    weight_ref[...] = weights
    for lo in range(0, cols, LANES):
        hi = lo + LANES
        quad = jnp.zeros((state, LANES), f32)
        for mask, ref in enumerate(refs):
            quad = quad + ref[:state, lo:hi].astype(f32) * weights[mask : mask + 1, lo:hi]
        quad_ref[:, lo:hi] = quad.astype(bf16)


def pair_kernel(
    dims, lengths, group, own_ref, one_ref, two_ref, three_ref, weight_ref, two_in,
    pair_ref, beside_ref, across_ref,
):
    (state,) = dims
    cols = pair_ref.shape[1]
    beside_ref[:state] = own_ref[:state]
    beside_ref[state : 2 * state] = two_in[:state]
    across_ref[state:] = three_ref[:state]
    for lo in range(0, cols, LANES):
        hi = lo + LANES
        pair = jnp.zeros((state, LANES), f32)
        for mask, ref in enumerate((own_ref, one_ref, two_ref, three_ref)):
            weight = weight_ref[PLACES + mask : PLACES + mask + 1, lo:hi]
            pair = pair + ref[:state, lo:hi].astype(f32) * weight
        pair = pair.astype(bf16)
        pair_ref[:, lo:hi] = pair
        across_ref[:state, lo:hi] = pair
        beside_ref[2 * state :, lo:hi] = pair


def with_head(patch, body):
    return jnp.concatenate([patch, body[HALO:]], axis=0)


def shared_kernel(
    dims, lengths, group, kq_ref, pkq_ref, cumt_ref, level_ref, entry_ref,
    queries_ref, scores_ref, parts_ref, coef_ref,
):
    tok, recordings, state, far_from = dims
    heads = entry_ref.shape[0]
    bounds = segment_bounds(lengths, recordings)
    first = group[0] * tok
    kq = with_head(pkq_ref[...], kq_ref[...])
    queries_ref[...] = kq[:, state:]
    s_pos = iota((tok, tok), 0)
    t_pos = iota((tok, tok), 1)
    valid = same_segment(first + s_pos, first + t_pos, bounds) * jnp.where(s_pos <= t_pos, 1.0, 0.0)
    scores_ref[...] = dot(kq[:, :state], kq[:, state:], ((1,), (1,))) * valid
    high, rest = two_parts(cumt_ref[...])
    mid, low = two_parts(rest)
    parts_ref[...] = jnp.concatenate([high, mid, low], axis=1).astype(bf16)
    for bit in range(coef_ref.shape[0]):
        coef = level_ref[far_from + bit] * entry_ref[...]
        coef = jnp.concatenate([coef, jnp.zeros((LANES - heads, tok), f32)], axis=0)
        coef_ref[bit] = jnp.transpose(coef)


def local_kernel(
    dims, mask, lengths, group, xs_ref, px_ref, scores_ref, cum_ref, parts_ref, level_ref, skip_ref,
    out_ref, mixing_ref, copied_ref,
):
    tok, head_dim, low_bits = dims
    cols = out_ref.shape[1]
    count = cols // head_dim
    quarter = jnp.bitwise_xor(lax.rem(group[0], PLACES), mask)
    first_head = quarter * count
    rows = 32
    row_bits = rows.bit_length() - 1
    where = pl.multiple_of(quarter * cols, LANES)
    copies = spread(LANES, first_head, count * LANES, LANES)
    copied_ref[...] = dot(parts_ref[...], jnp.concatenate([copies] * 3, axis=0), ((1,), (0,)))
    diff = jnp.bitwise_xor(iota((rows, tok), 0), lax.rem(iota((rows, tok), 1), rows))
    near = jnp.zeros((rows, tok), jnp.int32)
    for bit in range(row_bits):
        near = near + (diff >= 2**bit).astype(jnp.int32)
    token = iota((1, tok), 1) // rows
    lane = iota((1, 2 * head_dim), 1)
    unit = jnp.where(iota((tok, tok), 0) == iota((tok, tok), 1), 1.0, 0.0).astype(bf16)
    mixing_ref[...] = jnp.zeros(mixing_ref.shape, bf16)
    pieces = []
    for head in range(count):
        if head % 2 == 0:
            lo = head * head_dim
            here = pl.ds(pl.multiple_of(where + lo, LANES), 2 * head_dim)
            xs = with_head(px_ref[:, here], xs_ref[:, here])
            xst = jnp.transpose(xs)
        cum = cum_ref[pl.ds(first_head + head, 1), :]
        levels = [level_ref[level, pl.ds(first_head + head, 1), :] for level in range(low_bits + 1)]
        inner = jnp.broadcast_to(levels[0], (rows, tok))
        for level in range(1, row_bits + 1):
            inner = jnp.where(near == level, levels[level], inner)
        for s in range(0, tok, rows):
            at = s // rows
            outer = jnp.zeros((1, tok), f32)
            apart = jnp.bitwise_xor(token, at)
            for level in range(row_bits + 1, low_bits + 1):
                outer = jnp.where(apart >= 2 ** (level - row_bits - 1), levels[level], outer)
            before = copied_ref[s : s + rows, head * LANES : (head + 1) * LANES]
            for t in range(s // LANES * LANES, tok, LANES):
                here_t = slice(t, t + LANES)
                picked = outer[:, here_t]
                gap = cum[:, here_t] - before
                if t <= s:
                    picked = jnp.where(token[:, here_t] == at, inner[:, here_t], picked)
                    gap = jnp.minimum(gap, 0.0)
                mixing_ref[head % 2, s : s + rows, here_t] = (
                    jnp.exp(gap) * picked * scores_ref[s : s + rows, here_t]
                ).astype(bf16)
        pieces.append(
            dot(
                xst[head % 2 * head_dim : (head % 2 + 1) * head_dim],
                mixing_ref[head % 2],
                ((1,), (0,)),
            )
        )
        if head % 2 == 1:
            both = jnp.concatenate(pieces[-2:], axis=0)
            skip = jnp.where(
                lane < head_dim, skip_ref[first_head + head - 1], skip_ref[first_head + head]
            )
            out_ref[:, lo : lo + 2 * head_dim] = jnp.transpose(both) + skip * xs.astype(f32)


def far_kernel(
    dims, mask, lengths, group, sum_ref, queries_ref, coef_ref, scale_ref, low_ref,
    pair_ref, gate_ref, *refs,
):
    head_dim, state, low_from, pair_from = dims
    tok, cols = sum_ref.shape
    quarter = jnp.bitwise_xor(lax.rem(group[0], PLACES), mask)
    first = quarter * (cols // head_dim)
    queries = queries_ref[...]
    coefs = []
    for bit in range(coef_ref.shape[0]):
        on = jnp.where(lax.rem(group[0] // 2**bit, 2) == 1, 1.0, 0.0)
        coef = two_parts(coef_ref[bit] * (scale_ref[bit : bit + 1, :] * on))
        coefs.append(jnp.concatenate(coef, axis=1).astype(bf16))
    copies = spread(LANES, first, cols, head_dim)
    factors = dot(
        jnp.concatenate(coefs, axis=0), jnp.concatenate([copies, copies], axis=0), ((1,), (0,))
    )
    total = sum_ref[...]
    states = [low_ref[low_from : low_from + state], pair_ref[pair_from : pair_from + state]]
    if len(refs) > 2:
        states.append(refs[0][...])
    for bit, state_in in enumerate(states):
        total = total + dot(queries, state_in, ((1,), (0,))) * factors[bit * tok : (bit + 1) * tok]
    where = pl.multiple_of(quarter * cols, LANES)
    gate = silu(gate_ref[:, pl.ds(where, cols)].astype(f32))
    if len(refs) == 2:
        out_ref, next_ref = refs
        out_ref[...] = total * gate
        next_ref[...] = factors[2 * tok :] * gate
        return
    _, own_sum_ref, own_factor_ref, own_top_ref, out_ref, own_ref = refs
    out_ref[...] = total * gate
    read = dot(queries, own_top_ref[...], ((1,), (0,)))
    own_ref[...] = own_sum_ref[...] + read * own_factor_ref[...]


def final_kernel(
    dims, lengths, group, queries_ref, own_ref, done_ref, one_sum, one_factor, one_top, two_sum,
    two_factor, two_top, gain_ref, out_hbm, gated_ref, out_ref, sems,
):
    count, masks, chunks = dims
    place = lax.rem(group[0], PLACES)
    tok, cols = own_ref.shape
    queries = queries_ref[...]
    squares = jnp.zeros((tok, LANES), f32)
    for at, (total, factor, top) in enumerate(
        (
            (own_ref, None, None),
            (done_ref, None, None),
            (one_sum, one_factor, one_top),
            (two_sum, two_factor, two_top),
        )
    ):
        value = total[...]
        if top is not None:
            value = value + dot(queries, top[...], ((1,), (0,))) * factor[...]
            gated_ref[at - 2] = value
        for lo in range(0, cols, LANES):
            squares = squares + value[:, lo : lo + LANES] * value[:, lo : lo + LANES]
    mean = jnp.sum(squares, axis=1, keepdims=True) / count
    scale = lax.rsqrt(mean + eps_norm)
    rows = tok // chunks
    copies = []
    for chunk in range(chunks):
        here = slice(chunk * rows, (chunk + 1) * rows)
        for at, mask in enumerate(masks):
            where = pl.multiple_of(jnp.bitwise_xor(place, mask) * cols, LANES)
            value = (own_ref[here], done_ref[here])[at] if at < 2 else gated_ref[at - 2, here]
            out_ref[here, pl.ds(where, cols)] = (
                value * scale[here] * gain_ref[:, pl.ds(where, cols)]
            ).astype(bf16)
        copy = pltpu.make_async_copy(out_ref.at[here], out_hbm.at[here], sems.at[chunk])
        copy.start()
        copies.append(copy)
    for copy in copies:
        copy.wait()


VMEM = pl.BlockSpec(memory_space=pltpu.VMEM)
HBM = pl.BlockSpec(memory_space=pltpu.HBM)
SMEM = pl.BlockSpec(memory_space=pltpu.SMEM)


def call(
    kernel, scalars, operands, outs, scratch=(), flops=0, specs=None, out_specs=None, grid=(), mb=40, after=()
):
    moved = sum(a.size * a.dtype.itemsize for a in operands)
    moved += sum(o.size * o.dtype.itemsize for o in outs)
    specs = list(specs or [VMEM] * len(operands))
    first, last = len(scalars) + len(operands), len(scalars) + len(operands) + len(after)

    def body(*refs):
        kernel(*refs[:first], *refs[last:])

    return pl.pallas_call(
        body,
        grid=grid,
        in_specs=[SMEM] * len(scalars) + specs + [pl.BlockSpec(memory_space=pl.ANY)] * len(after),
        out_specs=out_specs or [VMEM] * len(outs),
        scratch_shapes=list(scratch),
        out_shape=outs,
        compiler_params=pltpu.CompilerParams(vmem_limit_bytes=mb * 2**20),
        cost_estimate=pl.CostEstimate(
            flops=flops, bytes_accessed=moved, transcendentals=0
        ),
    )(*scalars, *operands, *after)


def shape(dims, dtype):
    return jax.ShapeDtypeStruct(dims, dtype)


def per_device(
    mixed_input,
    conv_weight,
    conv_bias,
    gate_input,
    log_decay,
    level_weights,
    skip_gain,
    norm_gain,
    seg_lengths,
):
    tok, channels = mixed_input.shape
    width = gate_input.shape[1]
    heads = log_decay.shape[0]
    head_dim = width // heads
    state = (channels - width) // 2
    taps = conv_weight.shape[0]
    recordings = seg_lengths.shape[0]
    low_bits = tok.bit_length() - 1
    groups = lax.axis_size("group")
    high_bits = groups.bit_length() - 1
    group = lax.axis_index("group").astype(jnp.int32)
    place = group % PLACES
    cols = width // PLACES
    block = 2 * state
    levels = jnp.transpose(level_weights, (1, 0, 2))

    def send(value, pairs):
        return lax.ppermute(value, "group", pairs)

    def quad_send(value, mask, wanted=lambda source, target: True):
        pairs = [(g, g ^ mask) for g in range(groups) if wanted(g, g ^ mask)]
        return send(value, pairs)

    halo = send(mixed_input[tok - HALO :], [(g, (g + 1) % groups) for g in range(groups)])

    def in_hbm(value):
        return pltpu.with_memory_space_constraint(value, pltpu.HBM)

    xs, kq, part, cum, cumt, entry, head, weights, first, lengths = call(
        functools.partial(
            features_kernel, (tok, heads, head_dim, taps, recordings, width, state)
        ),
        (group[None],),
        (
            in_hbm(mixed_input),
            in_hbm(conv_weight),
            in_hbm(conv_bias),
            in_hbm(log_decay),
            in_hbm(seg_lengths),
        ),
        [
            shape((tok, width), bf16),
            shape((tok, block), bf16),
            shape((state, width), f32),
            shape((heads, tok), f32),
            shape((tok, LANES), f32),
            shape((heads, tok), f32),
            shape((HALO, channels), bf16),
            shape((8, channels), f32),
            shape((HALO, width), f32),
            shape((recordings,), jnp.int32),
        ],
        [
            pltpu.VMEM((tok, channels), bf16),
            pltpu.VMEM((heads, tok), f32),
            pltpu.VMEM(((taps - 1) * tok, tok), bf16),
            pltpu.VMEM((tok, width), bf16),
            pltpu.SemaphoreType.DMA((5,)),
        ],
        flops=2 * tok * width * state,
        specs=[HBM] * 5,
        out_specs=[VMEM] * 9 + [SMEM],
    )
    scalars = (lengths, group[None])

    payload = shape((state + HALO, cols), bf16)
    px, pkq, own, one, two, three = call(
        functools.partial(join_kernel, (tok, taps, recordings, width, state)),
        scalars,
        (halo, head, weights, first, cumt, part),
        [shape((HALO, width), bf16), shape((HALO, block), bf16)] + [payload] * PLACES,
        [pltpu.VMEM((HALO, width), bf16)],
        flops=2 * HALO * width * state,
    )

    queries, scores, parts, coefs = call(
        functools.partial(shared_kernel, (tok, recordings, state, low_bits + 1)),
        scalars,
        (kq, pkq, cumt, levels, entry),
        [
            shape((tok, state), bf16),
            shape((tok, tok), f32),
            shape((tok, 3 * LANES), bf16),
            shape((3, tok, LANES), f32),
        ],
        flops=2 * tok * tok * state,
    )

    def local(mask, after=()):
        return call(
            functools.partial(local_kernel, (tok, head_dim, low_bits), mask),
            scalars,
            (xs, px, scores, cum, parts, levels, skip_gain),
            [shape((tok, cols), f32)],
            [pltpu.VMEM((2, tok, tok), bf16), pltpu.VMEM((tok, cols // head_dim * LANES), f32)],
            specs=[VMEM] * 6 + [SMEM],
            flops=2 * cols * tok * tok,
            after=after,
        )[0]

    got_three = quad_send(three, 3)
    got_one = quad_send(one, 1)
    got_two = quad_send(two, 2)
    sums = [local(0), local(1)]
    received = (own, got_one, got_two, got_three)
    quad, scale, spread_weights = call(
        functools.partial(combine_kernel, (state, head_dim)),
        scalars,
        received,
        [shape((state, cols), bf16), shape((8, LANES), f32), shape((8, cols), f32)],
        flops=4 * state * cols,
        after=sums,
    )
    pair, beside, across = call(
        functools.partial(pair_kernel, (state,)),
        scalars,
        received + (spread_weights, two),
        [
            shape((state, cols), bf16),
            shape((3 * state, cols), bf16),
            shape((2 * state, cols), bf16),
        ],
        flops=4 * state * cols,
        after=(quad,),
    )
    sums.append(local(2, (quad,)))
    sums.append(local(3, ()))
    got_three_of_pair = quad_send(pair, 3, lambda source, target: target & 2)
    got_beside = quad_send(beside, 1)
    got_across = quad_send(across, 2)

    lows = [(got_one, 0), (got_beside, 0), (got_across, state), (got_beside, state)]
    pairs = [(pair, 0), (got_beside, 2 * state), (got_across, 0), (got_three_of_pair, 0)]

    def far_part(mask, more=(), after=()):
        return list(
            call(
                functools.partial(far_kernel, (head_dim, state, lows[mask][1], pairs[mask][1]), mask),
                scalars,
                (sums[mask], queries, coefs, scale, lows[mask][0], pairs[mask][0], gate_input) + more,
                [shape((tok, cols), f32), shape((tok, cols), f32)],
                flops=int(2 * 1.1e9),
                after=after,
            )
        )

    halves = {0: far_part(0)}

    befores = [scale[0, :heads], scale[1, :heads], scale[2, :heads]]
    crossed = []
    running, total = quad, scale[3, :heads]
    for bit in range(2, high_bits):
        mask = 2**bit
        last = bit + 1 == high_bits
        far = quad_send(running, mask, lambda source, target: True)
        crossed.append(lax.optimization_barrier((far, sums[3], sums[2], halves[0][0]))[0])
        if not last:
            on_top = group // mask % 2 == 1
            far_total = quad_send(total, mask)

            def columns(value):
                mine = lax.dynamic_slice(value, (place * (cols // head_dim),), (cols // head_dim,))
                return jnp.repeat(mine, head_dim)[None, :]

            running = jnp.where(
                on_top,
                far.astype(f32) * columns(total) + running.astype(f32),
                running.astype(f32) * columns(far_total) + far.astype(f32),
            ).astype(bf16)
            befores.append(jnp.where(on_top, far_total * befores[-1], befores[-1]))
            total = total * far_total

    def all_quarters(value, bit):
        return [value] + [
            quad_send(value, mask)
            for mask in range(1, PLACES)
        ]

    tops = [all_quarters(value, bit + 2) for bit, value in enumerate(crossed)]
    halves[2] = far_part(2)
    halves[1] = far_part(1, after=halves[2][:1])
    extra = {mask: [] for mask in range(PLACES)}
    for bit in range(3, high_bits):
        coef = levels[low_bits + 1 + bit] * entry
        coef = coef * jnp.where(group // 2**bit % 2 == 1, befores[bit], 0.0)[:, None]
        for mask in range(PLACES):
            first_head = (place ^ mask) * (cols // head_dim)
            mine = lax.dynamic_slice_in_dim(coef, first_head, cols // head_dim, axis=0)
            gate = lax.dynamic_slice_in_dim(gate_input, (place ^ mask) * cols, cols, axis=1)
            read = jnp.dot(queries, tops[bit - 2][mask], preferred_element_type=f32)
            read = read * jnp.repeat(mine, head_dim, axis=0).T
            extra[mask].append(read * jax.nn.silu(gate.astype(f32)))
    for mask in halves:
        halves[mask][0] = sum(extra[mask], halves[mask][0])
    done, own_done = far_part(3, (tops[0][3], halves[0][0], halves[0][1], tops[0][0]), halves[1][:1])
    done = sum(extra[3], done)

    chunks = 4
    return call(
        functools.partial(final_kernel, (float(width), (0, 3, 1, 2), chunks)),
        scalars,
        (
            queries,
            own_done,
            done,
            halves[1][0],
            halves[1][1],
            tops[0][1],
            halves[2][0],
            halves[2][1],
            tops[0][2],
            norm_gain[None, :],
        ),
        [shape((tok, width), bf16)],
        [
            pltpu.VMEM((2, tok, cols), f32),
            pltpu.VMEM((tok, width), bf16),
            pltpu.SemaphoreType.DMA((chunks,)),
        ],
        out_specs=[HBM],
        flops=2 * tok * width * state,
    )[0]


def solution(mesh):
    in_specs = (
        P(("batch", "group"), None),
        P(),
        P(),
        P(("batch", "group"), None),
        P(None, ("batch", "group")),
        P(None, None, ("batch", "group")),
        P(),
        P(),
        P("batch"),
    )
    out_specs = P(("batch", "group"), None)
    return jax.shard_map(
        per_device, mesh=mesh, in_specs=in_specs, out_specs=out_specs, check_vma=False
    )
```
